512 devices in a mesh: day: 64 (over z, y), pair: 8 (over x, core).
Axes of the slice: x: 4, y: 4, z: 16, core: 2. Of those that a mesh axis runs over, the one named last changes fastest.
Arguments:
- spectra: bfloat16 [128, 128, 4096], P('day', 'pair'), may hold values from -40 to 40
- pair_stations: int32 [512, 2], P('pair'), may hold values from 0 to 127
- availability: int32 [128, 128], P('day'), may hold values from 0 to 1
Outputs:
- stacks: bfloat16 [128, 512, 1001], P('day', 'pair')
- reference: float32 [512, 1001], P('pair')
The draws below stay inside these ranges and needn't reach their ends.
All inputs are finite; a program needn't handle non-finite values.
Results may differ from the reference program's by a relative error of at most 0.008.
Values may be sent and summed in bfloat16 or wider, within the bound.
A program may use at most 64 MiB of HBM per device.

```python
import math
import jax
import jax.numpy as jnp
from jax import lax

BINS = 2048
LAGS = 1001
WINDOW = 30
DAYS = 128
PAIRS = 512
STATIONS = 128


def draw_spectra(key, part):
    key_noise, key_station, key_band = jax.random.split(key, 3)
    station_scale = jnp.exp(jax.random.uniform(key_station, (1, STATIONS, 1)) * math.log(10.0))
    band_half = jnp.exp(jax.random.uniform(key_band, (1, 1, BINS)) * math.log(10.0))
    band_scale = jnp.concatenate([band_half, band_half], 2)
    noise = jnp.clip(jax.random.normal(key_noise, (DAYS, STATIONS, 2 * BINS)), -6.0, 6.0)
    values = noise * station_scale * band_scale / 21.5
    return values.astype(jnp.bfloat16)


def draw_availability(key, part):
    draws = jax.random.randint(key, (DAYS, STATIONS), 0, 1000)
    level = 300 + 650 * jnp.arange(DAYS, dtype=jnp.int32) // DAYS
    return (draws < level[:, None]).astype(jnp.int32)


def place_ends(array, key, low, top_value):
    place = [jax.random.randint(jax.random.fold_in(key, axis), (), 0, length) for axis, length in enumerate(array.shape)]
    widest = array.shape.index(max(array.shape))
    neighbour = place[:widest] + [(place[widest] + 1) % array.shape[widest]] + place[widest + 1:]
    return array.at[tuple(place)].set(low).at[tuple(neighbour)].set(top_value)


def setup_inputs(seed: int = 0) -> dict:
    key_list = jax.random.split(jax.random.key(seed), 4)
    spectra = draw_spectra(jax.random.fold_in(key_list[3], 71), 0)
    pair_stations = place_ends(jax.random.randint(key_list[1], (PAIRS, 2), 0, STATIONS), jax.random.fold_in(key_list[1], 1), 0, STATIONS - 1).astype(jnp.int32)
    availability = draw_availability(jax.random.fold_in(key_list[3], 71), 0)
    return dict(spectra=spectra, pair_stations=pair_stations, availability=availability)


def lag_table(bin_count, lag_count):
    bin_ids = jnp.arange(bin_count, dtype=jnp.int32)[:, None]
    lag_ids = jnp.arange(lag_count, dtype=jnp.int32)[None, :] - (lag_count - 1) // 2
    phase_ids = jnp.mod(bin_ids * lag_ids, 2 * bin_count)
    angle = phase_ids.astype(jnp.float32) * jnp.float32(2.0 * math.pi / (2 * bin_count))
    factor = jnp.float32(1.0 / math.sqrt(2 * bin_count))
    return jnp.concatenate([jnp.cos(angle) * factor, -jnp.sin(angle) * factor], 0).astype(jnp.bfloat16)

def reference(spectra, pair_stations, availability):
    inverse = lag_table(BINS, LAGS).astype(jnp.float32)
    station_one = pair_stations[:, 0].astype(jnp.int32)
    station_two = pair_stations[:, 1].astype(jnp.int32)

    def one_day(items):
        spec_day, avail_day = items
        first_spec = jnp.take(spec_day, station_one, axis=0).astype(jnp.float32)
        second_spec = jnp.take(spec_day, station_two, axis=0).astype(jnp.float32)
        real_one, imag_one = (first_spec[:, :BINS], first_spec[:, BINS:])
        real_two, imag_two = (second_spec[:, :BINS], second_spec[:, BINS:])
        real_part = real_one * real_two + imag_one * imag_two
        imag_part = real_one * imag_two - imag_one * real_two
        cross = jnp.concatenate([real_part, imag_part], 1).astype(jnp.bfloat16)
        present = (jnp.take(avail_day, station_one) * jnp.take(avail_day, station_two)).astype(jnp.float32)
        corr = jnp.dot(cross.astype(jnp.float32), inverse, precision=lax.Precision.HIGHEST)
        return ((corr * present[:, None]).astype(jnp.bfloat16), present)
    daily, present = lax.map(one_day, (spectra, availability))
    daily_wide = daily.astype(jnp.float32)
    moving = lax.reduce_window(daily_wide, jnp.zeros((), daily_wide.dtype), lax.add, (WINDOW, 1, 1), (1, 1, 1), [(WINDOW - 1, 0), (0, 0), (0, 0)])
    counts = lax.reduce_window(present, jnp.zeros((), present.dtype), lax.add, (WINDOW, 1), (1, 1), [(WINDOW - 1, 0), (0, 0)])
    ref_stack = lax.optimization_barrier(jnp.sum(daily_wide, axis=0)) / DAYS
    scale = jnp.sqrt(lax.optimization_barrier(jnp.mean(ref_stack * ref_stack, axis=1)) + 1e-06)
    stacks = moving / jnp.maximum(counts, 1.0)[:, :, None] / scale[None, :, None]
    return (stacks.astype(jnp.bfloat16), ref_stack)
```

```python
import jax
import jax.numpy as jnp
import numpy as np
from jax import lax
from jax.sharding import PartitionSpec as P

LAGS = 1001
WIDE = 1024
WINDOW = 30


def lag_table(bin_count):
    bin_ids = np.arange(bin_count)[:, None]
    lag_ids = np.arange(LAGS)[None, :] - (LAGS - 1) // 2
    angle = np.mod(bin_ids * lag_ids, 2 * bin_count) * (np.pi / bin_count)
    factor = 1.0 / np.sqrt(2.0 * bin_count)
    table = np.concatenate([np.cos(angle) * factor, -np.sin(angle) * factor], 0)
    return np.pad(table, ((0, 0), (0, WIDE - LAGS))).astype(np.float32).astype(jnp.bfloat16)


def per_device(spectra, pair_stations, availability):
    days_here = spectra.shape[0]
    groups = lax.axis_size("day")
    station_count = spectra.shape[1] * lax.axis_size("pair")
    bin_count = spectra.shape[2] // 2
    pairs_here = pair_stations.shape[0]
    inverse = jnp.asarray(lag_table(bin_count))
    station_ids = jnp.arange(station_count, dtype=jnp.int32)
    ends = jnp.concatenate([pair_stations[:, 0], pair_stations[:, 1]], 0)
    pick = (ends[:, None] == station_ids[None, :]).astype(jnp.bfloat16)
    avail = jnp.dot(availability.astype(jnp.bfloat16), pick.T, preferred_element_type=jnp.float32)
    present = avail[:, :pairs_here] * avail[:, pairs_here:]
    gathered = lax.all_gather(spectra, "pair", axis=1, tiled=True)
    rows = []
    for day in range(days_here):
        spec = jnp.dot(pick, gathered[day], preferred_element_type=jnp.float32)
        one, two = spec[:pairs_here], spec[pairs_here:]
        ar, ai, br, bi = one[:, :bin_count], one[:, bin_count:], two[:, :bin_count], two[:, bin_count:]
        rows.append(jnp.concatenate([ar * br + ai * bi, ar * bi - ai * br], 1).astype(jnp.bfloat16))
    cross = jnp.concatenate(rows, 0)
    corr = jnp.dot(cross, inverse, preferred_element_type=jnp.float32)
    column = lax.broadcasted_iota(jnp.int32, (1, WIDE), 1)
    shown = present.reshape(-1, 1)
    daily = jnp.where(column == LAGS, shown, corr * shown).astype(jnp.bfloat16)
    daily = daily.reshape(days_here, pairs_here, WIDE)
    turned = lax.all_to_all(daily, "day", split_axis=1, concat_axis=0, tiled=True)
    days = groups * days_here
    mine = turned.reshape(days, WIDE)
    day_ids = np.arange(days)
    gap = day_ids[:, None] - day_ids[None, :]
    band = jnp.asarray(((gap >= 0) & (gap < WINDOW)).astype(np.float32), dtype=jnp.bfloat16)
    moving = jnp.dot(band, mine, preferred_element_type=jnp.float32)
    counts = moving[:, LAGS:LAGS + 1]
    ref = jnp.sum(mine.astype(jnp.float32), axis=0) / days
    ref = jnp.where(column[0] < LAGS, ref, 0.0)
    scale = jnp.sqrt(jnp.sum(ref * ref) / LAGS + 1e-06)
    stacks = (moving / jnp.maximum(counts, 1.0) / scale).astype(jnp.bfloat16)
    back = lax.all_to_all(stacks.reshape(days, 1, WIDE), "day", split_axis=0, concat_axis=1, tiled=True)
    ref_all = lax.all_gather(ref[None], "day", axis=0, tiled=True)
    return back[:, :, :LAGS], ref_all[:, :LAGS]


def solution(mesh):
    return jax.shard_map(
        per_device,
        mesh=mesh,
        in_specs=(P("day", "pair", None), P("pair", None), P("day", None)),
        out_specs=(P("day", "pair", None), P("pair", None)),
        check_vma=False,
    )
```

```python
import functools

import jax
import jax.numpy as jnp
import numpy as np
from jax import lax
from jax.experimental import pallas as pl
from jax.experimental.pallas import tpu as pltpu
from jax.sharding import PartitionSpec as P

LAGS = 1001
WIDE = 1024
TILES = WIDE // 128
WINDOW = 30
ALONG_X = 4
ALONG_Y = 4
BLOCK = 16
PAD = 16
F32 = jnp.float32
BF16 = jnp.bfloat16


def lag_table(bin_count):
    bin_ids = np.arange(bin_count)[:, None]
    lag_ids = np.arange(LAGS)[None, :] - (LAGS - 1) // 2
    angle = np.mod(bin_ids * lag_ids, 2 * bin_count) * (np.pi / bin_count)
    factor = 1.0 / np.sqrt(2.0 * bin_count)
    table = np.concatenate([np.cos(angle) * factor, -np.sin(angle) * factor], 0)
    return np.pad(table, ((0, 0), (0, WIDE - LAGS))).astype(np.float32).astype(jnp.bfloat16)


def rows(index, count=BLOCK):
    return pl.ds(pl.multiple_of(index * count, count), count)


def kernel(groups, days, spectra, ends, availability, table_hbm, stacks, reference,
           gathered, table, cross, spread, daily, turned, held, ready, back, refs,
           odd_pad, sum_pad, two_pad, four_pad, eight_pad,
           table_sem, own_sem, give, take, day_sems):
    me = lax.axis_index("day")
    mine = lax.axis_index("pair")
    x, core = mine // 2, mine % 2
    z, y = me // ALONG_Y, me % ALONG_Y
    planes = groups // ALONG_Y
    right = ((x + 1) % ALONG_X) * 2 + core
    left = ((x + ALONG_X - 1) % ALONG_X) * 2 + core
    across = ((x + 2) % ALONG_X) * 2 + core
    sibling = x * 2 + 1 - core
    bins2 = spectra.shape[2]
    half = bins2 // 2

    barrier = pltpu.get_barrier_semaphore()
    for other in (right, left, sibling):
        pl.semaphore_signal(barrier, inc=1, device_id={"pair": other}, device_id_type=pl.DeviceIdType.MESH)

    def greet(i, carry):
        pl.semaphore_signal(barrier, inc=1, device_id={"day": (me + i) % groups}, device_id_type=pl.DeviceIdType.MESH)
        return carry

    lax.fori_loop(1, groups, greet, 0)
    table_copy = pltpu.make_async_copy(table_hbm, table, table_sem)
    table_copy.start()
    own_copy = pltpu.make_async_copy(spectra, gathered.at[:, rows(mine)], own_sem)
    own_copy.start()
    pl.semaphore_wait(barrier, groups + 2)

    def to(kind, day, src, dst, other):
        copy = pltpu.make_async_remote_copy(
            src_ref=src, dst_ref=dst, send_sem=give.at[kind, day], recv_sem=take.at[kind, day],
            device_id={"pair": other}, device_id_type=pl.DeviceIdType.MESH)
        copy.start()
        return copy

    first = []
    for day in range(2):
        place = gathered.at[day, rows(mine)]
        first.append((to(0, day, spectra.at[day], place, right),
                      to(1, day, spectra.at[day], place, left),
                      to(2, day, spectra.at[day], place, sibling)))

    for pad in (odd_pad, sum_pad, two_pad, four_pad, eight_pad):
        pad[0:PAD] = jnp.zeros((PAD, 8, 128), F32)
    pairs = ends.shape[1]
    station = lax.broadcasted_iota(jnp.int32, (128, pairs), 0)
    pick_one = jnp.where(station == ends[0:1, :], 1.0, 0.0).astype(F32).T
    pick_two = jnp.where(station == ends[1:2, :], 1.0, 0.0).astype(F32).T
    pick = jnp.concatenate([pick_one, pick_two], 0).astype(BF16)
    shown = []
    for day in range(2):
        there = availability[day:day + 1, :].astype(F32)
        shown.append(jnp.sum(pick_one * there, axis=1, keepdims=True) * jnp.sum(pick_two * there, axis=1, keepdims=True))

    second, third = [], []
    for day in range(2):
        from_left, from_right, from_sibling = first[day]
        part = gathered.at[day, rows(left)]
        from_left.wait_recv()
        ahead = to(3, day, part.at[:, 0:half], part.at[:, 0:half], right)
        down = to(4, day, part, part, sibling)
        part = gathered.at[day, rows(right)]
        from_right.wait_recv()
        second.append((ahead, to(5, day, part.at[:, half:], part.at[:, half:], left), down, to(6, day, part, part, sibling)))
    own_copy.wait()
    for day in range(2):
        from_left, from_right, down_one, down_two = second[day]
        part = gathered.at[day, rows(across)]
        from_left.wait_recv()
        one = to(7, day, part.at[:, 0:half], part.at[:, 0:half], sibling)
        from_right.wait_recv()
        two = to(8, day, part.at[:, half:], part.at[:, half:], sibling)
        third.append((one, two))
        for copy in (first[day][2], down_one, down_two, one, two):
            copy.wait_recv()
        width = min(512, half)
        for at in range(0, half, width):
            real = jnp.dot(pick, gathered[day, :, at:at + width], preferred_element_type=F32)
            imag = jnp.dot(pick, gathered[day, :, half + at:half + at + width], preferred_element_type=F32)
            ar, br, ai, bi = real[:pairs], real[pairs:], imag[:pairs], imag[pairs:]
            cross[day * pairs:(day + 1) * pairs, at:at + width] = (ar * br + ai * bi).astype(BF16)
            cross[day * pairs:(day + 1) * pairs, half + at:half + at + width] = (ar * bi - ai * br).astype(BF16)
    table_copy.wait()
    spare = lax.broadcasted_iota(jnp.int32, (pairs, 128), 1) == LAGS - 128 * (TILES - 1)
    for at in range(0, WIDE, 256):
        corr = jnp.dot(cross[...], table[:, at:at + 256], preferred_element_type=F32)
        for day in range(2):
            for j in range(2):
                tile = at // 128 + j
                part = corr[day * pairs:(day + 1) * pairs, 128 * j:128 * (j + 1)] * shown[day]
                if tile == TILES - 1:
                    part = jnp.where(spare, shown[day], part)
                spread[pl.ds(8 * day + tile, pairs, stride=BLOCK), :] = part
    daily[...] = spread[...].astype(BF16)

    def turn(src, dst, send_sem, recv_sem):
        def copy(to_group):
            return pltpu.make_async_remote_copy(
                src_ref=src.at[rows(to_group)], dst_ref=dst.at[rows(me)], send_sem=send_sem, recv_sem=recv_sem,
                device_id={"day": to_group}, device_id_type=pl.DeviceIdType.MESH)

        def step(i, carry):
            copy((me + i) % groups).start()
            copy((me + groups - i) % groups).start()
            return carry

        lax.fori_loop(1, groups // 2, step, 0)
        copy((me + groups // 2) % groups).start()
        count = (groups - 1) * BLOCK
        return pltpu.make_async_remote_copy(
            src_ref=src.at[0:count], dst_ref=dst.at[0:count], send_sem=send_sem, recv_sem=recv_sem,
            device_id={"day": (me + 1) % groups}, device_id_type=pl.DeviceIdType.MESH)

    there = turn(daily, turned, day_sems.at[0], day_sems.at[1])
    turned[rows(me), :] = daily[rows(me), :]
    there.wait_recv()

    blocks = turned[...].astype(F32).reshape(groups, BLOCK, 128)
    even, odd = blocks[:, :8], blocks[:, 8:]
    both = even + odd
    own = slice(PAD, PAD + groups)

    def past(ref, by):
        return ref[PAD - by:PAD - by + groups]

    odd_pad[own] = odd
    sum_pad[own] = both
    two = both + past(sum_pad, 1)
    two_pad[own] = two
    four = two + past(two_pad, 2)
    four_pad[own] = four
    eight_pad[own] = four + past(four_pad, 4)
    full = past(eight_pad, 1) + past(four_pad, 9) + past(two_pad, 13)
    ref_row = jnp.sum(both, axis=0) / days
    lag = 128 * lax.broadcasted_iota(jnp.int32, (8, 128), 0) + lax.broadcasted_iota(jnp.int32, (8, 128), 1)
    power = jnp.sum(jnp.where(lag < LAGS, ref_row * ref_row, 0.0), axis=(0, 1), keepdims=True) / LAGS
    scale = jnp.sqrt(power + 1e-06)[None]
    refs[z, rows(y, 8), :] = ref_row

    def along_z(plane):
        return pltpu.make_async_remote_copy(
            src_ref=refs.at[z, rows(y, 8)], dst_ref=refs.at[z, rows(y, 8)], send_sem=day_sems.at[4], recv_sem=day_sems.at[5],
            device_id={"day": plane * ALONG_Y + y}, device_id_type=pl.DeviceIdType.MESH)

    def step_z(i, carry):
        along_z((z + i) % planes).start()
        return carry

    lax.fori_loop(1, planes, step_z, 0)
    spot = LAGS - 128 * (TILES - 1)

    def normalised(moving):
        counts = moving[:, 7:8, spot:spot + 1]
        return moving * (1.0 / (jnp.maximum(counts, 1.0) * scale))

    ready[...] = jnp.concatenate(
        [normalised(full + past(odd_pad, 15) + even), normalised(full + both)], 1).reshape(groups * BLOCK, 128).astype(BF16)
    home = turn(ready, back, day_sems.at[2], day_sems.at[3])
    back[rows(me), :] = ready[rows(me), :]

    got_z = pltpu.make_async_remote_copy(
        src_ref=refs.at[0:planes - 1, 0:8], dst_ref=refs.at[0:planes - 1, 0:8], send_sem=day_sems.at[4], recv_sem=day_sems.at[5],
        device_id={"day": ((z + 1) % planes) * ALONG_Y + y}, device_id_type=pl.DeviceIdType.MESH)
    got_z.wait_recv()
    for i in range(1, ALONG_Y):
        pltpu.make_async_remote_copy(
            src_ref=refs.at[:, rows(y, 8)], dst_ref=refs.at[:, rows(y, 8)], send_sem=day_sems.at[6], recv_sem=day_sems.at[7],
            device_id={"day": z * ALONG_Y + (y + i) % ALONG_Y}, device_id_type=pl.DeviceIdType.MESH).start()
    got_y = pltpu.make_async_remote_copy(
        src_ref=refs.at[:, 0:24], dst_ref=refs.at[:, 0:24], send_sem=day_sems.at[6], recv_sem=day_sems.at[7],
        device_id={"day": z * ALONG_Y + (y + 1) % ALONG_Y}, device_id_type=pl.DeviceIdType.MESH)
    got_y.wait_recv()
    held[...] = refs[...].reshape(groups * 8, 128)
    for tile in range(TILES):
        wide = min(128, LAGS - 128 * tile)
        reference[:, 128 * tile:128 * tile + wide] = held[pl.ds(tile, groups, stride=8), :][:, :wide]

    home.wait_recv()
    spread[...] = back[...].astype(F32)
    for day in range(2):
        for tile in range(TILES):
            wide = min(128, LAGS - 128 * tile)
            part = spread[pl.ds(8 * day + tile, groups, stride=BLOCK), :].astype(BF16)
            stacks[day, :, 128 * tile:128 * tile + wide] = part[:, :wide]

    for day in range(2):
        for copy in first[day] + second[day] + third[day]:
            copy.wait_send()
    there.wait_send()
    home.wait_send()
    got_z.wait_send()
    got_y.wait_send()


def per_device(spectra, pair_stations, availability):
    groups = lax.axis_size("day")
    days_here, shard, bins2 = spectra.shape
    stations = shard * lax.axis_size("pair")
    pairs = pair_stations.shape[0]
    table = jnp.asarray(lag_table(bins2 // 2))
    vmem = pl.BlockSpec(memory_space=pltpu.VMEM)
    anywhere = pl.BlockSpec(memory_space=pl.ANY)
    padded = pltpu.VMEM((PAD + groups, 8, 128), F32)
    block = pltpu.VMEM((groups * BLOCK, 128), BF16)
    return pl.pallas_call(
        functools.partial(kernel, groups, groups * days_here),
        out_shape=(jax.ShapeDtypeStruct((days_here, pairs, LAGS), BF16), jax.ShapeDtypeStruct((pairs, LAGS), F32)),
        in_specs=[anywhere, vmem, vmem, anywhere],
        out_specs=(vmem, vmem),
        scratch_shapes=[
            pltpu.VMEM((days_here, stations, bins2), BF16),
            pltpu.VMEM((bins2, WIDE), BF16),
            pltpu.VMEM((days_here * pairs, bins2), BF16),
            pltpu.VMEM((groups * BLOCK, 128), F32),
            block, block,
            pltpu.VMEM((groups * 8, 128), F32),
            block, block,
            pltpu.VMEM((groups // ALONG_Y, ALONG_Y * 8, 128), F32),
            padded, padded, padded, padded, padded,
            pltpu.SemaphoreType.DMA,
            pltpu.SemaphoreType.DMA,
            pltpu.SemaphoreType.DMA((9, 2)),
            pltpu.SemaphoreType.DMA((9, 2)),
            pltpu.SemaphoreType.DMA((8,)),
        ],
        compiler_params=pltpu.CompilerParams(
            collective_id=0, has_side_effects=True, vmem_limit_bytes=48 * 2**20),
    )(spectra, pair_stations.T, availability, table)


def solution(mesh):
    return jax.shard_map(
        per_device,
        mesh=mesh,
        in_specs=(P("day", "pair", None), P("pair", None), P("day", None)),
        out_specs=(P("day", "pair", None), P("pair", None)),
        check_vma=False,
    )
```

```python
import functools

import jax
import jax.numpy as jnp
import numpy as np
from jax import lax
from jax.experimental import pallas as pl
from jax.experimental.pallas import tpu as pltpu
from jax.sharding import PartitionSpec as P

LAGS = 1001
WIDE = 1024
TILES = WIDE // 128
WINDOW = 30
ALONG_X = 4
ALONG_Y = 4
BLOCK = 16
PAD = 16
F32 = jnp.float32
BF16 = jnp.bfloat16
MESH = pl.DeviceIdType.MESH
SPOT = LAGS - 128 * (TILES - 1)
VMEM_LIMIT = 58 * 2**20


def lag_table(bin_count):
    bin_ids = np.arange(bin_count)[:, None]
    lag_ids = np.arange(LAGS)[None, :] - (LAGS - 1) // 2
    angle = np.mod(bin_ids * lag_ids, 2 * bin_count) * (np.pi / bin_count)
    factor = 1.0 / np.sqrt(2.0 * bin_count)
    table = np.concatenate([np.cos(angle) * factor, -np.sin(angle) * factor], 0)
    return np.pad(table, ((0, 0), (0, WIDE - LAGS))).astype(np.float32).astype(jnp.bfloat16)


def rows(index, count=BLOCK):
    return pl.ds(pl.multiple_of(index * count, count), count)


def kernel(groups, days, spectra, ends_hbm, availability_hbm, table_hbm, back, refs,
           gathered, table, cross, spread, daily, turned, ready, ends, availability,
           odd_pad, sum_pad, two_pad, four_pad, eight_pad,
           local_sems, give, take, day_sems):
    me = lax.axis_index("day")
    mine = lax.axis_index("pair")
    x, core = mine // 2, mine % 2
    z, y = me // ALONG_Y, me % ALONG_Y
    planes = groups // ALONG_Y
    right = ((x + 1) % ALONG_X) * 2 + core
    left = ((x + ALONG_X - 1) % ALONG_X) * 2 + core
    across = ((x + 2) % ALONG_X) * 2 + core
    sibling = x * 2 + 1 - core
    half = spectra.shape[2] // 2
    pairs = ends.shape[1]
    far = groups // 2

    barrier = pltpu.get_barrier_semaphore()

    def greet(i, carry):
        pl.semaphore_signal(barrier, inc=1, device_id={"day": (me + i) % groups}, device_id_type=MESH)
        return carry

    lax.fori_loop(1, groups, greet, 0)
    for other in (right, left, sibling):
        pl.semaphore_signal(barrier, inc=1, device_id={"pair": other}, device_id_type=MESH)
    own_copy = pltpu.make_async_copy(spectra, gathered.at[:, rows(mine)], local_sems.at[0])
    own_copy.start()
    ends_copy = pltpu.make_async_copy(ends_hbm, ends, local_sems.at[1])
    ends_copy.start()
    availability_copy = pltpu.make_async_copy(availability_hbm, availability, local_sems.at[2])
    availability_copy.start()
    table_copy = pltpu.make_async_copy(table_hbm, table, local_sems.at[3])
    table_copy.start()
    for pad in (odd_pad, sum_pad, two_pad, four_pad, eight_pad):
        pad[0:PAD] = jnp.zeros((PAD, 8, 128), F32)
    pl.semaphore_wait(barrier, groups + 2)

    sent = []

    def to(kind, day, src, dst, other):
        copy = pltpu.make_async_remote_copy(
            src_ref=src, dst_ref=dst, send_sem=give.at[kind, day], recv_sem=take.at[kind, day],
            device_id={"pair": other}, device_id_type=MESH)
        copy.start()
        sent.append(copy)
        return copy

    def block(day, who):
        return gathered.at[day, rows(who)]

    def send_own(day):
        return (to(0, day, spectra.at[day], block(day, mine), right), to(1, day, spectra.at[day], block(day, mine), left),
                to(2, day, spectra.at[day], block(day, mine), sibling))

    def pass_on(day, own):
        part = block(day, left)
        own[0].wait_recv()
        ahead = to(3, day, part.at[:, 0:half], part.at[:, 0:half], right)
        other = block(day, right)
        own[1].wait_recv()
        return (ahead, to(5, day, other.at[:, half:], other.at[:, half:], left),
                to(4, day, part, part, sibling), to(6, day, other, other, sibling))

    def pass_down(day, own, passed):
        part = block(day, across)
        passed[0].wait_recv()
        one = to(7, day, part.at[:, 0:half], part.at[:, 0:half], sibling)
        passed[1].wait_recv()
        two = to(8, day, part.at[:, half:], part.at[:, half:], sibling)
        for copy in (own[2], passed[2], passed[3], one, two):
            copy.wait_recv()

    def cross_of(day):
        width = min(512, half)
        for at in range(0, half, width):
            real = jnp.dot(pick, gathered[day, :, at:at + width], preferred_element_type=F32)
            imag = jnp.dot(pick, gathered[day, :, half + at:half + at + width], preferred_element_type=F32)
            ar, br, ai, bi = real[:pairs], real[pairs:], imag[:pairs], imag[pairs:]
            cross[:, at:at + width] = (ar * br + ai * bi).astype(BF16)
            cross[:, half + at:half + at + width] = (ar * bi - ai * br).astype(BF16)

    def daily_of(day):
        shown = present[day]
        spare = lax.broadcasted_iota(jnp.int32, (pairs, 128), 1) == SPOT
        for at in range(0, WIDE, 256):
            corr = jnp.dot(cross[...], table[:, at:at + 256], preferred_element_type=F32)
            for j in range(2):
                tile = at // 128 + j
                part = corr[:, 128 * j:128 * (j + 1)] * shown
                if tile == TILES - 1:
                    part = jnp.where(spare, shown, part)
                spread[pl.ds(tile, pairs, stride=8), :] = part
        daily[day] = spread[...].reshape(groups, 8, 128).astype(BF16)

    def turn(here, there, send_sem, recv_sem):
        def copy(to_group):
            return pltpu.make_async_remote_copy(
                src_ref=here(to_group, 1), dst_ref=there(me, 1), send_sem=send_sem, recv_sem=recv_sem,
                device_id={"day": to_group}, device_id_type=MESH)

        copy((me + far) % groups).start()

        def step(i, carry):
            copy((me + far + i) % groups).start()
            copy((me + far - i) % groups).start()
            return carry

        lax.fori_loop(1, far, step, 0)
        return pltpu.make_async_remote_copy(
            src_ref=here(0, groups - 1), dst_ref=there(0, groups - 1), send_sem=send_sem, recv_sem=recv_sem,
            device_id={"day": (me + 1) % groups}, device_id_type=MESH)

    def turn_day(day):
        copies = turn(lambda i, n: daily.at[day, pl.ds(i, n)], lambda i, n: turned.at[day, pl.ds(i, n)],
                      day_sems.at[0, day], day_sems.at[1, day])
        turned[day, pl.ds(me, 1)] = daily[day, pl.ds(me, 1)]
        return copies

    own_zero = send_own(0)
    ends_copy.wait()
    availability_copy.wait()
    station = lax.broadcasted_iota(jnp.int32, (128, pairs), 0)
    pick_one = jnp.where(station == ends[0:1, :], 1.0, 0.0).astype(F32).T
    pick_two = jnp.where(station == ends[1:2, :], 1.0, 0.0).astype(F32).T
    pick = jnp.concatenate([pick_one, pick_two], 0).astype(BF16)
    present = []
    for day in range(2):
        up = availability[day:day + 1, :].astype(F32)
        present.append(jnp.sum(pick_one * up, axis=1, keepdims=True) * jnp.sum(pick_two * up, axis=1, keepdims=True))
    own_copy.wait()

    passed_zero = pass_on(0, own_zero)
    own_one = send_own(1)
    pass_down(0, own_zero, passed_zero)
    cross_of(0)
    passed_one = pass_on(1, own_one)
    table_copy.wait()
    daily_of(0)
    turn_zero = turn_day(0)
    pass_down(1, own_one, passed_one)
    cross_of(1)
    daily_of(1)
    turn_one = turn_day(1)
    turn_zero.wait_recv()
    turn_one.wait_recv()

    even, odd = turned[0].astype(F32), turned[1].astype(F32)
    both = even + odd
    ref_row = jnp.sum(both, axis=0) / days
    refs[z, rows(y, 8), :] = ref_row

    def along_z(plane):
        return pltpu.make_async_remote_copy(
            src_ref=refs.at[z, rows(y, 8)], dst_ref=refs.at[z, rows(y, 8)], send_sem=day_sems.at[0, 2], recv_sem=day_sems.at[1, 2],
            device_id={"day": plane * ALONG_Y + y}, device_id_type=MESH)

    def step_z(i, carry):
        along_z((z + i) % planes).start()
        return carry

    lax.fori_loop(1, planes, step_z, 0)
    own = slice(PAD, PAD + groups)

    def past(ref, by):
        return ref[PAD - by:PAD - by + groups]

    odd_pad[own] = odd
    sum_pad[own] = both
    two = both + past(sum_pad, 1)
    two_pad[own] = two
    four = two + past(two_pad, 2)
    four_pad[own] = four
    eight_pad[own] = four + past(four_pad, 4)
    full = past(eight_pad, 1) + past(four_pad, 9) + past(two_pad, 13)
    lag = 128 * lax.broadcasted_iota(jnp.int32, (8, 128), 0) + lax.broadcasted_iota(jnp.int32, (8, 128), 1)
    power = jnp.sum(jnp.where(lag < LAGS, ref_row * ref_row, 0.0), axis=(0, 1), keepdims=True) / LAGS
    scale = jnp.sqrt(power + 1e-06)[None]

    def normalised(moving):
        counts = moving[:, 7:8, SPOT:SPOT + 1]
        return moving * (1.0 / (jnp.maximum(counts, 1.0) * scale))

    ready[...] = jnp.concatenate(
        [normalised(full + past(odd_pad, 15) + even), normalised(full + both)], 1).reshape(groups * BLOCK, 128).astype(BF16)
    home = turn(lambda i, n: ready.at[pl.ds(pl.multiple_of(i * BLOCK, BLOCK), n * BLOCK)],
                lambda i, n: back.at[pl.ds(pl.multiple_of(i * BLOCK, BLOCK), n * BLOCK)],
                day_sems.at[0, 3], day_sems.at[1, 3])
    back[rows(me), :] = ready[rows(me), :]

    got_z = pltpu.make_async_remote_copy(
        src_ref=refs.at[0:planes - 1, 0:8], dst_ref=refs.at[0:planes - 1, 0:8], send_sem=day_sems.at[0, 2], recv_sem=day_sems.at[1, 2],
        device_id={"day": ((z + 1) % planes) * ALONG_Y + y}, device_id_type=MESH)
    got_z.wait_recv()
    for i in range(1, ALONG_Y):
        pltpu.make_async_remote_copy(
            src_ref=refs.at[:, rows(y, 8)], dst_ref=refs.at[:, rows(y, 8)], send_sem=day_sems.at[0, 4], recv_sem=day_sems.at[1, 4],
            device_id={"day": z * ALONG_Y + (y + i) % ALONG_Y}, device_id_type=MESH).start()
    got_y = pltpu.make_async_remote_copy(
        src_ref=refs.at[:, 0:24], dst_ref=refs.at[:, 0:24], send_sem=day_sems.at[0, 4], recv_sem=day_sems.at[1, 4],
        device_id={"day": z * ALONG_Y + (y + 1) % ALONG_Y}, device_id_type=MESH)
    got_y.wait_recv()
    for copy in sent:
        copy.wait_send()
    turn_zero.wait_send()
    turn_one.wait_send()
    got_z.wait_send()
    got_y.wait_send()
    home.wait_recv()
    home.wait_send()


def lay_out(back, refs, stacks_hbm, reference_hbm, spread, held, stacks, reference, sems):
    groups = held.shape[0] // 8
    held[...] = refs[...].reshape(groups * 8, 128)
    for tile in range(TILES):
        wide = min(128, LAGS - 128 * tile)
        reference[:, 128 * tile:128 * tile + wide] = held[pl.ds(tile, groups, stride=8), :][:, :wide]
    copies = [pltpu.make_async_copy(reference, reference_hbm, sems.at[2])]
    copies[0].start()
    spread[...] = back[...].astype(F32)
    for day in range(2):
        for tile in range(TILES):
            wide = min(128, LAGS - 128 * tile)
            part = spread[pl.ds(8 * day + tile, groups, stride=BLOCK), :].astype(BF16)
            stacks[day, :, 128 * tile:128 * tile + wide] = part[:, :wide]
        copies.append(pltpu.make_async_copy(stacks.at[day], stacks_hbm.at[day], sems.at[day]))
        copies[-1].start()
    for copy in copies:
        copy.wait()


def per_device(spectra, pair_stations, availability):
    groups = lax.axis_size("day")
    days_here, shard, bins2 = spectra.shape
    stations = shard * lax.axis_size("pair")
    pairs = pair_stations.shape[0]
    table = jnp.asarray(lag_table(bins2 // 2))
    vmem = pl.BlockSpec(memory_space=pltpu.VMEM)
    anywhere = pl.BlockSpec(memory_space=pl.ANY)
    padded = pltpu.VMEM((PAD + groups, 8, 128), F32)
    by_day = pltpu.VMEM((days_here, groups, 8, 128), BF16)
    dma = pltpu.SemaphoreType.DMA
    back, refs = pl.pallas_call(
        functools.partial(kernel, groups, groups * days_here),
        out_shape=(pltpu.VMEM((groups * BLOCK, 128), BF16),
                   pltpu.VMEM((groups // ALONG_Y, ALONG_Y * 8, 128), F32)),
        in_specs=[anywhere] * 4,
        out_specs=(vmem, vmem),
        scratch_shapes=[
            pltpu.VMEM((days_here, stations, bins2), BF16),
            pltpu.VMEM((bins2, WIDE), BF16),
            pltpu.VMEM((pairs, bins2), BF16),
            pltpu.VMEM((groups * 8, 128), F32),
            by_day, by_day,
            pltpu.VMEM((groups * BLOCK, 128), BF16),
            pltpu.VMEM((2, pairs), jnp.int32),
            pltpu.VMEM((days_here, stations), jnp.int32),
            padded, padded, padded, padded, padded,
            dma((4,)), dma((9, 2)), dma((9, 2)), dma((2, 5)),
        ],
        compiler_params=pltpu.CompilerParams(
            collective_id=0, has_side_effects=True, vmem_limit_bytes=VMEM_LIMIT),
    )(spectra, pair_stations.T, availability, table)
    return pl.pallas_call(
        lay_out,
        out_shape=(jax.ShapeDtypeStruct((days_here, pairs, LAGS), BF16), jax.ShapeDtypeStruct((pairs, LAGS), F32)),
        in_specs=[vmem, vmem],
        out_specs=(anywhere, anywhere),
        scratch_shapes=[
            pltpu.VMEM((groups * BLOCK, 128), F32),
            pltpu.VMEM((groups * 8, 128), F32),
            pltpu.VMEM((days_here, pairs, LAGS), BF16),
            pltpu.VMEM((pairs, LAGS), F32),
            dma((3,)),
        ],
        compiler_params=pltpu.CompilerParams(vmem_limit_bytes=8 * 2**20),
    )(back, refs)


def solution(mesh):
    return jax.shard_map(
        per_device,
        mesh=mesh,
        in_specs=(P("day", "pair", None), P("pair", None), P("day", None)),
        out_specs=(P("day", "pair", None), P("pair", None)),
        check_vma=False,
    )
```

```python
import functools

import jax
import jax.numpy as jnp
import numpy as np
from jax import lax
from jax.experimental import pallas as pl
from jax.experimental.pallas import tpu as pltpu
from jax.sharding import PartitionSpec as P

LAGS = 1001
WIDE = 1024
TILES = WIDE // 128
WINDOW = 30
ALONG_X = 4
ALONG_Y = 4
BLOCK = 16
PAD = 16
F32 = jnp.float32
BF16 = jnp.bfloat16
MESH = pl.DeviceIdType.MESH
SPOT = LAGS - 128 * (TILES - 1)
VMEM_LIMIT = 58 * 2**20


def lag_table(bin_count):
    bin_ids = np.arange(bin_count)[:, None]
    lag_ids = np.arange(LAGS)[None, :] - (LAGS - 1) // 2
    angle = np.mod(bin_ids * lag_ids, 2 * bin_count) * (np.pi / bin_count)
    factor = 1.0 / np.sqrt(2.0 * bin_count)
    table = np.concatenate([np.cos(angle) * factor, -np.sin(angle) * factor], 0)
    return np.pad(table, ((0, 0), (0, WIDE - LAGS))).astype(np.float32).astype(jnp.bfloat16)


def rows(index, count=BLOCK):
    return pl.ds(pl.multiple_of(index * count, count), count)


def kernel(groups, days, spectra, ends_hbm, availability_hbm, table_hbm, back, refs,
           gathered, table, cross, handed, spread, daily, turned, ready, ends, availability,
           odd_pad, sum_pad, two_pad, four_pad, eight_pad,
           local_sems, give, take, day_sems):
    me = lax.axis_index("day")
    mine = lax.axis_index("pair")
    x, core = mine // 2, mine % 2
    z, y = me // ALONG_Y, me % ALONG_Y
    planes = groups // ALONG_Y
    sibling = x * 2 + 1 - core
    half = spectra.shape[2] // 2
    part = half // 2
    pairs = ends.shape[2]
    far = groups // 2

    barrier = pltpu.get_barrier_semaphore()

    def greet(i, carry):
        pl.semaphore_signal(barrier, inc=1, device_id={"day": (me + i) % groups}, device_id_type=MESH)
        return carry

    def at_offset(step, flip):
        return ((x + step) % ALONG_X) * 2 + (1 - core if flip else core)

    offsets = [(step, flip) for step in (1, 3, 2, 0) for flip in (False, True) if step or flip]
    for step, flip in offsets:
        pl.semaphore_signal(barrier, inc=1, device_id={"pair": at_offset(step, flip)}, device_id_type=MESH)
    lax.fori_loop(1, groups, greet, 0)

    def bins(which, kind):
        return pl.ds(pl.multiple_of(which * part + kind * half, 128), part)

    own_copies = []
    for kind in range(2):
        for day in range(2):
            own_copies.append(pltpu.make_async_copy(
                spectra.at[day, :, bins(core, kind)], gathered.at[day, rows(mine), kind * part:(kind + 1) * part],
                local_sems.at[4 + 2 * kind + day]))
            own_copies[-1].start()
    ends_copy = pltpu.make_async_copy(ends_hbm, ends.at[0], local_sems.at[1])
    ends_copy.start()
    availability_copy = pltpu.make_async_copy(availability_hbm, availability, local_sems.at[2])
    availability_copy.start()
    table_copy = pltpu.make_async_copy(table_hbm, table, local_sems.at[3])
    table_copy.start()
    for pad in (odd_pad, sum_pad, two_pad, four_pad, eight_pad):
        pad[0:PAD] = jnp.zeros((PAD, 8, 128), F32)
    pl.semaphore_wait(barrier, groups - 1 + len(offsets))

    sent = []

    def to(src, dst, send_sem, recv_sem, other):
        copy = pltpu.make_async_remote_copy(
            src_ref=src, dst_ref=dst, send_sem=send_sem, recv_sem=recv_sem,
            device_id={"pair": other}, device_id_type=MESH)
        copy.start()
        sent.append(copy)
        return copy

    def send_own(day):
        copies = []
        for number, (step, flip) in enumerate(offsets):
            for kind in range(2):
                copies.append(to(
                    spectra.at[day, :, bins(1 - core if flip else core, kind)],
                    gathered.at[day, rows(mine), kind * part:(kind + 1) * part],
                    give.at[2 * number + kind, day], take.at[2 * number + kind, day], at_offset(step, flip)))
        return copies

    def cross_of(day):
        copies = []
        width = min(512, part)
        for number, at in enumerate(range(0, part, width)):
            real = jnp.dot(pick, gathered[day, :, at:at + width], preferred_element_type=F32)
            imag = jnp.dot(pick, gathered[day, :, part + at:part + at + width], preferred_element_type=F32)
            ar, br, ai, bi = real[:2 * pairs], real[2 * pairs:], imag[:2 * pairs], imag[2 * pairs:]
            for kind, made in enumerate(((ar * br + ai * bi).astype(BF16), (ar * bi - ai * br).astype(BF16))):
                place = pl.ds(pl.multiple_of(core * part + kind * half + at, 128), width)
                handed[day, :, kind * part + at:kind * part + at + width] = made[pairs:]
                cross[day, :, place] = made[:pairs]
                copies.append(to(
                    handed.at[day, :, kind * part + at:kind * part + at + width], cross.at[day, :, place],
                    give.at[14 + 2 * number + kind, day], take.at[14 + 2 * number + kind, day], sibling))
        return copies

    def daily_of(day):
        shown = present[day]
        spare = lax.broadcasted_iota(jnp.int32, (pairs, 128), 1) == SPOT
        for at in range(0, WIDE, 256):
            corr = jnp.dot(cross[day], table[:, at:at + 256], preferred_element_type=F32)
            for j in range(2):
                tile = at // 128 + j
                piece = corr[:, 128 * j:128 * (j + 1)] * shown
                if tile == TILES - 1:
                    piece = jnp.where(spare, shown, piece)
                spread[pl.ds(tile, pairs, stride=8), :] = piece
        daily[day] = spread[...].reshape(groups, 8, 128).astype(BF16)

    def turn(here, there, send_sem, recv_sem):
        def copy(to_group):
            return pltpu.make_async_remote_copy(
                src_ref=here(to_group, 1), dst_ref=there(me, 1), send_sem=send_sem, recv_sem=recv_sem,
                device_id={"day": to_group}, device_id_type=MESH)

        copy((me + far) % groups).start()

        def step(i, carry):
            copy((me + far + i) % groups).start()
            copy((me + far - i) % groups).start()
            return carry

        lax.fori_loop(1, far, step, 0)
        return pltpu.make_async_remote_copy(
            src_ref=here(0, groups - 1), dst_ref=there(0, groups - 1), send_sem=send_sem, recv_sem=recv_sem,
            device_id={"day": (me + 1) % groups}, device_id_type=MESH)

    def turn_day(day):
        copies = turn(lambda i, n: daily.at[day, pl.ds(i, n)], lambda i, n: turned.at[day, pl.ds(i, n)],
                      day_sems.at[0, day], day_sems.at[1, day])
        turned[day, pl.ds(me, 1)] = daily[day, pl.ds(me, 1)]
        return copies

    own_zero = send_own(0)
    ends_copy.wait()
    met = to(ends.at[0], ends.at[1], local_sems.at[0], local_sems.at[8], sibling)
    own_one = send_own(1)
    availability_copy.wait()
    met.wait_recv()
    station = lax.broadcasted_iota(jnp.int32, (128, pairs), 0)

    def picks(end):
        return [jnp.where(station == ends[who, end:end + 1, :], 1.0, 0.0).astype(F32).T for who in range(2)]

    pick_one, pick_two = picks(0), picks(1)
    pick = jnp.concatenate(pick_one + pick_two, 0).astype(BF16)
    present = []
    for day in range(2):
        up = availability[day:day + 1, :].astype(F32)
        present.append(jnp.sum(pick_one[0] * up, axis=1, keepdims=True) * jnp.sum(pick_two[0] * up, axis=1, keepdims=True))
    for copy in own_copies:
        copy.wait()
    for copy in own_zero:
        copy.wait_recv()
    halves_zero = cross_of(0)
    table_copy.wait()
    for copy in halves_zero:
        copy.wait_recv()
    daily_of(0)
    turn_zero = turn_day(0)
    for copy in own_one:
        copy.wait_recv()
    for copy in cross_of(1):
        copy.wait_recv()
    daily_of(1)
    turn_one = turn_day(1)
    turn_zero.wait_recv()
    turn_one.wait_recv()

    even, odd = turned[0].astype(F32), turned[1].astype(F32)
    both = even + odd
    ref_row = jnp.sum(both, axis=0) / days
    refs[z, rows(y, 8), :] = ref_row

    def along_z(plane):
        return pltpu.make_async_remote_copy(
            src_ref=refs.at[z, rows(y, 8)], dst_ref=refs.at[z, rows(y, 8)], send_sem=day_sems.at[0, 2], recv_sem=day_sems.at[1, 2],
            device_id={"day": plane * ALONG_Y + y}, device_id_type=MESH)

    def step_z(i, carry):
        along_z((z + i) % planes).start()
        return carry

    lax.fori_loop(1, planes, step_z, 0)
    own = slice(PAD, PAD + groups)

    def past(ref, by):
        return ref[PAD - by:PAD - by + groups]

    odd_pad[own] = odd
    sum_pad[own] = both
    two = both + past(sum_pad, 1)
    two_pad[own] = two
    four = two + past(two_pad, 2)
    four_pad[own] = four
    eight_pad[own] = four + past(four_pad, 4)
    full = past(eight_pad, 1) + past(four_pad, 9) + past(two_pad, 13)
    lag = 128 * lax.broadcasted_iota(jnp.int32, (8, 128), 0) + lax.broadcasted_iota(jnp.int32, (8, 128), 1)
    power = jnp.sum(jnp.where(lag < LAGS, ref_row * ref_row, 0.0), axis=(0, 1), keepdims=True) / LAGS
    scale = jnp.sqrt(power + 1e-06)[None]

    def normalised(moving):
        counts = moving[:, 7:8, SPOT:SPOT + 1]
        return moving * (1.0 / (jnp.maximum(counts, 1.0) * scale))

    ready[...] = jnp.concatenate(
        [normalised(full + past(odd_pad, 15) + even), normalised(full + both)], 1).reshape(groups * BLOCK, 128).astype(BF16)
    home = turn(lambda i, n: ready.at[pl.ds(pl.multiple_of(i * BLOCK, BLOCK), n * BLOCK)],
                lambda i, n: back.at[pl.ds(pl.multiple_of(i * BLOCK, BLOCK), n * BLOCK)],
                day_sems.at[0, 3], day_sems.at[1, 3])
    back[rows(me), :] = ready[rows(me), :]

    got_z = pltpu.make_async_remote_copy(
        src_ref=refs.at[0:planes - 1, 0:8], dst_ref=refs.at[0:planes - 1, 0:8], send_sem=day_sems.at[0, 2], recv_sem=day_sems.at[1, 2],
        device_id={"day": ((z + 1) % planes) * ALONG_Y + y}, device_id_type=MESH)
    got_z.wait_recv()
    for i in range(1, ALONG_Y):
        pltpu.make_async_remote_copy(
            src_ref=refs.at[:, rows(y, 8)], dst_ref=refs.at[:, rows(y, 8)], send_sem=day_sems.at[0, 4], recv_sem=day_sems.at[1, 4],
            device_id={"day": z * ALONG_Y + (y + i) % ALONG_Y}, device_id_type=MESH).start()
    got_y = pltpu.make_async_remote_copy(
        src_ref=refs.at[:, 0:24], dst_ref=refs.at[:, 0:24], send_sem=day_sems.at[0, 4], recv_sem=day_sems.at[1, 4],
        device_id={"day": z * ALONG_Y + (y + 1) % ALONG_Y}, device_id_type=MESH)
    got_y.wait_recv()
    for copy in sent:
        copy.wait_send()
    turn_zero.wait_send()
    turn_one.wait_send()
    got_z.wait_send()
    got_y.wait_send()
    home.wait_recv()
    home.wait_send()


def lay_out(back, refs, stacks_hbm, reference_hbm, spread, held, stacks, reference, sems):
    groups = held.shape[0] // 8
    held[...] = refs[...].reshape(groups * 8, 128)
    for tile in range(TILES):
        wide = min(128, LAGS - 128 * tile)
        reference[:, 128 * tile:128 * tile + wide] = held[pl.ds(tile, groups, stride=8), :][:, :wide]
    copies = [pltpu.make_async_copy(reference, reference_hbm, sems.at[2])]
    copies[0].start()
    spread[...] = back[...].astype(F32)
    for day in range(2):
        for tile in range(TILES):
            wide = min(128, LAGS - 128 * tile)
            part = spread[pl.ds(8 * day + tile, groups, stride=BLOCK), :].astype(BF16)
            stacks[day, :, 128 * tile:128 * tile + wide] = part[:, :wide]
        copies.append(pltpu.make_async_copy(stacks.at[day], stacks_hbm.at[day], sems.at[day]))
        copies[-1].start()
    for copy in copies:
        copy.wait()


def per_device(spectra, pair_stations, availability):
    groups = lax.axis_size("day")
    days_here, shard, bins2 = spectra.shape
    stations = shard * lax.axis_size("pair")
    pairs = pair_stations.shape[0]
    table = jnp.asarray(lag_table(bins2 // 2))
    vmem = pl.BlockSpec(memory_space=pltpu.VMEM)
    anywhere = pl.BlockSpec(memory_space=pl.ANY)
    padded = pltpu.VMEM((PAD + groups, 8, 128), F32)
    by_day = pltpu.VMEM((days_here, groups, 8, 128), BF16)
    dma = pltpu.SemaphoreType.DMA
    back, refs = pl.pallas_call(
        functools.partial(kernel, groups, groups * days_here),
        out_shape=(pltpu.VMEM((groups * BLOCK, 128), BF16),
                   pltpu.VMEM((groups // ALONG_Y, ALONG_Y * 8, 128), F32)),
        in_specs=[anywhere] * 4,
        out_specs=(vmem, vmem),
        scratch_shapes=[
            pltpu.VMEM((days_here, stations, bins2 // 2), BF16),
            pltpu.VMEM((bins2, WIDE), BF16),
            pltpu.VMEM((days_here, pairs, bins2), BF16),
            pltpu.VMEM((days_here, pairs, bins2 // 2), BF16),
            pltpu.VMEM((groups * 8, 128), F32),
            by_day, by_day,
            pltpu.VMEM((groups * BLOCK, 128), BF16),
            pltpu.VMEM((2, 2, pairs), jnp.int32),
            pltpu.VMEM((days_here, stations), jnp.int32),
            padded, padded, padded, padded, padded,
            dma((9,)), dma((18, 2)), dma((18, 2)), dma((2, 5)),
        ],
        compiler_params=pltpu.CompilerParams(
            collective_id=0, has_side_effects=True, vmem_limit_bytes=VMEM_LIMIT),
    )(spectra, pair_stations.T, availability, table)
    return pl.pallas_call(
        lay_out,
        out_shape=(jax.ShapeDtypeStruct((days_here, pairs, LAGS), BF16), jax.ShapeDtypeStruct((pairs, LAGS), F32)),
        in_specs=[vmem, vmem],
        out_specs=(anywhere, anywhere),
        scratch_shapes=[
            pltpu.VMEM((groups * BLOCK, 128), F32),
            pltpu.VMEM((groups * 8, 128), F32),
            pltpu.VMEM((days_here, pairs, LAGS), BF16),
            pltpu.VMEM((pairs, LAGS), F32),
            dma((3,)),
        ],
        compiler_params=pltpu.CompilerParams(vmem_limit_bytes=8 * 2**20),
    )(back, refs)


def solution(mesh):
    return jax.shard_map(
        per_device,
        mesh=mesh,
        in_specs=(P("day", "pair", None), P("pair", None), P("day", None)),
        out_specs=(P("day", "pair", None), P("pair", None)),
        check_vma=False,
    )
```

```python
import functools

import jax
import jax.numpy as jnp
import numpy as np
from jax import lax
from jax.experimental import pallas as pl
from jax.experimental.pallas import tpu as pltpu
from jax.sharding import PartitionSpec as P

LAGS = 1001
WIDE = 1024
TILES = WIDE // 128
WINDOW = 30
ALONG_X = 4
ALONG_Y = 4
BLOCK = 16
PAD = 16
F32 = jnp.float32
BF16 = jnp.bfloat16
MESH = pl.DeviceIdType.MESH
SPOT = LAGS - 128 * (TILES - 1)
VMEM_LIMIT = 58 * 2**20


def lag_table(bin_count):
    bin_ids = np.arange(bin_count)[:, None]
    lag_ids = np.arange(LAGS)[None, :] - (LAGS - 1) // 2
    angle = np.mod(bin_ids * lag_ids, 2 * bin_count) * (np.pi / bin_count)
    factor = 1.0 / np.sqrt(2.0 * bin_count)
    table = np.concatenate([np.cos(angle) * factor, -np.sin(angle) * factor], 0)
    return np.pad(table, ((0, 0), (0, WIDE - LAGS))).astype(np.float32).astype(jnp.bfloat16)


def rows(index, count=BLOCK):
    return pl.ds(pl.multiple_of(index * count, count), count)


def kernel(groups, days, spectra, ends_hbm, availability_hbm, table_hbm, back, refs,
           gathered, table, cross, handed, spread, daily, turned, ready, ends, availability,
           odd_pad, sum_pad, two_pad, four_pad, eight_pad,
           local_sems, give, take, day_sems):
    me = lax.axis_index("day")
    mine = lax.axis_index("pair")
    x, core = mine // 2, mine % 2
    z, y = me // ALONG_Y, me % ALONG_Y
    planes = groups // ALONG_Y
    sibling = x * 2 + 1 - core
    half = spectra.shape[2] // 2
    part = half // 2
    pairs = ends.shape[2]
    far = groups // 2

    barrier = pltpu.get_barrier_semaphore()

    def greet(i, carry):
        pl.semaphore_signal(barrier, inc=1, device_id={"day": (me + i) % groups}, device_id_type=MESH)
        return carry

    def at_offset(step, flip):
        return ((x + step) % ALONG_X) * 2 + (1 - core if flip else core)

    offsets = [(step, flip) for step in (1, 3, 2, 0) for flip in (False, True) if step or flip]
    for step, flip in offsets:
        pl.semaphore_signal(barrier, inc=1, device_id={"pair": at_offset(step, flip)}, device_id_type=MESH)
    lax.fori_loop(1, groups, greet, 0)

    def bins(which, kind):
        return pl.ds(pl.multiple_of(which * part + kind * half, 128), part)

    own_copies = []
    for kind in range(2):
        for day in range(2):
            own_copies.append(pltpu.make_async_copy(
                spectra.at[day, :, bins(core, kind)], gathered.at[day, rows(mine), kind * part:(kind + 1) * part],
                local_sems.at[4 + 2 * kind + day]))
            own_copies[-1].start()
    ends_copy = pltpu.make_async_copy(ends_hbm, ends.at[0], local_sems.at[1])
    ends_copy.start()
    availability_copy = pltpu.make_async_copy(availability_hbm, availability, local_sems.at[2])
    availability_copy.start()
    table_copy = pltpu.make_async_copy(table_hbm, table, local_sems.at[3])
    table_copy.start()
    for pad in (odd_pad, sum_pad, two_pad, four_pad, eight_pad):
        pad[0:PAD] = jnp.zeros((PAD, 8, 128), F32)
    pl.semaphore_wait(barrier, groups - 1 + len(offsets))

    sent = []

    def to(src, dst, send_sem, recv_sem, other):
        copy = pltpu.make_async_remote_copy(
            src_ref=src, dst_ref=dst, send_sem=send_sem, recv_sem=recv_sem,
            device_id={"pair": other}, device_id_type=MESH)
        copy.start()
        sent.append(copy)
        return copy

    def send_own(day):
        copies = []
        for number, (step, flip) in enumerate(offsets):
            for kind in range(2):
                copies.append(to(
                    spectra.at[day, :, bins(1 - core if flip else core, kind)],
                    gathered.at[day, rows(mine), kind * part:(kind + 1) * part],
                    give.at[2 * number + kind, day], take.at[2 * number + kind, day], at_offset(step, flip)))
        return copies

    def cross_of(day):
        copies = []
        width = min(512, part)
        for number, at in enumerate(range(0, part, width)):
            real = jnp.dot(pick, gathered[day, :, at:at + width], preferred_element_type=F32)
            imag = jnp.dot(pick, gathered[day, :, part + at:part + at + width], preferred_element_type=F32)
            ar, br, ai, bi = real[:2 * pairs], real[2 * pairs:], imag[:2 * pairs], imag[2 * pairs:]
            for kind, made in enumerate(((ar * br + ai * bi).astype(BF16), (ar * bi - ai * br).astype(BF16))):
                place = pl.ds(pl.multiple_of(core * part + kind * half + at, 128), width)
                handed[day, :, kind * part + at:kind * part + at + width] = made[pairs:]
                cross[day, :, place] = made[:pairs]
                copies.append(to(
                    handed.at[day, :, kind * part + at:kind * part + at + width], cross.at[day, :, place],
                    give.at[14 + 2 * number + kind, day], take.at[14 + 2 * number + kind, day], sibling))
        return copies

    def daily_of(day):
        shown = present[day]
        spare = lax.broadcasted_iota(jnp.int32, (pairs, 128), 1) == SPOT
        for at in range(0, WIDE, 256):
            corr = jnp.dot(cross[day], table[:, at:at + 256], preferred_element_type=F32)
            for j in range(2):
                tile = at // 128 + j
                piece = corr[:, 128 * j:128 * (j + 1)] * shown
                if tile == TILES - 1:
                    piece = jnp.where(spare, shown, piece)
                spread[pl.ds(tile, pairs, stride=8), :] = piece
        daily[day] = spread[...].reshape(groups, 8, 128).astype(BF16)

    def turn(here, there, send_sem, recv_sem):
        def copy(to_group):
            return pltpu.make_async_remote_copy(
                src_ref=here(to_group, 1), dst_ref=there(me, 1), send_sem=send_sem, recv_sem=recv_sem,
                device_id={"day": to_group}, device_id_type=MESH)

        copy((me + far) % groups).start()

        def step(i, carry):
            copy((me + far + i) % groups).start()
            copy((me + far - i) % groups).start()
            return carry

        lax.fori_loop(1, far, step, 0)
        return pltpu.make_async_remote_copy(
            src_ref=here(0, groups - 1), dst_ref=there(0, groups - 1), send_sem=send_sem, recv_sem=recv_sem,
            device_id={"day": (me + 1) % groups}, device_id_type=MESH)

    def turn_day(day):
        copies = turn(lambda i, n: daily.at[day, pl.ds(i, n)], lambda i, n: turned.at[day, pl.ds(i, n)],
                      day_sems.at[0, day], day_sems.at[1, day])
        turned[day, pl.ds(me, 1)] = daily[day, pl.ds(me, 1)]
        return copies

    own_zero = send_own(0)
    ends_copy.wait()
    met = to(ends.at[0], ends.at[1], local_sems.at[0], local_sems.at[8], sibling)
    availability_copy.wait()
    met.wait_recv()
    station = lax.broadcasted_iota(jnp.int32, (128, pairs), 0)

    def picks(end):
        return [jnp.where(station == ends[who, end:end + 1, :], 1.0, 0.0).astype(F32).T for who in range(2)]

    pick_one, pick_two = picks(0), picks(1)
    pick = jnp.concatenate(pick_one + pick_two, 0).astype(BF16)
    present = []
    for day in range(2):
        up = availability[day:day + 1, :].astype(F32)
        present.append(jnp.sum(pick_one[0] * up, axis=1, keepdims=True) * jnp.sum(pick_two[0] * up, axis=1, keepdims=True))
    for copy in own_zero:
        copy.wait_send()
    sent.clear()
    sent.append(met)
    own_one = send_own(1)
    for copy in own_copies:
        copy.wait()
    for copy in own_zero:
        copy.wait_recv()
    halves_zero = cross_of(0)
    table_copy.wait()
    for copy in halves_zero:
        copy.wait_recv()
    daily_of(0)
    turn_zero = turn_day(0)
    for copy in own_one:
        copy.wait_recv()
    for copy in cross_of(1):
        copy.wait_recv()
    daily_of(1)
    turn_one = turn_day(1)
    turn_zero.wait_recv()
    turn_one.wait_recv()

    even, odd = turned[0].astype(F32), turned[1].astype(F32)
    both = even + odd
    ref_row = jnp.sum(both, axis=0) / days
    refs[pl.ds(z, 1), pl.ds(y, 1)] = ref_row.astype(BF16)[None, None]

    def along_z(plane):
        return pltpu.make_async_remote_copy(
            src_ref=refs.at[pl.ds(z, 1), pl.ds(y, 1)], dst_ref=refs.at[pl.ds(z, 1), pl.ds(y, 1)], send_sem=day_sems.at[0, 2], recv_sem=day_sems.at[1, 2],
            device_id={"day": plane * ALONG_Y + y}, device_id_type=MESH)

    def step_z(i, carry):
        along_z((z + i) % planes).start()
        return carry

    lax.fori_loop(1, planes, step_z, 0)
    own = slice(PAD, PAD + groups)

    def past(ref, by):
        return ref[PAD - by:PAD - by + groups]

    odd_pad[own] = odd
    sum_pad[own] = both
    two = both + past(sum_pad, 1)
    two_pad[own] = two
    four = two + past(two_pad, 2)
    four_pad[own] = four
    eight_pad[own] = four + past(four_pad, 4)
    full = past(eight_pad, 1) + past(four_pad, 9) + past(two_pad, 13)
    lag = 128 * lax.broadcasted_iota(jnp.int32, (8, 128), 0) + lax.broadcasted_iota(jnp.int32, (8, 128), 1)
    power = jnp.sum(jnp.where(lag < LAGS, ref_row * ref_row, 0.0), axis=(0, 1), keepdims=True) / LAGS
    scale = jnp.sqrt(power + 1e-06)[None]

    def normalised(moving):
        counts = moving[:, 7:8, SPOT:SPOT + 1]
        return moving * (1.0 / (jnp.maximum(counts, 1.0) * scale))

    ready[...] = jnp.concatenate(
        [normalised(full + past(odd_pad, 15) + even), normalised(full + both)], 1).reshape(groups * BLOCK, 128).astype(BF16)
    home = turn(lambda i, n: ready.at[pl.ds(pl.multiple_of(i * BLOCK, BLOCK), n * BLOCK)],
                lambda i, n: back.at[pl.ds(pl.multiple_of(i * BLOCK, BLOCK), n * BLOCK)],
                day_sems.at[0, 3], day_sems.at[1, 3])
    back[rows(me), :] = ready[rows(me), :]

    got_z = pltpu.make_async_remote_copy(
        src_ref=refs.at[0:planes - 1, 0:1], dst_ref=refs.at[0:planes - 1, 0:1], send_sem=day_sems.at[0, 2], recv_sem=day_sems.at[1, 2],
        device_id={"day": ((z + 1) % planes) * ALONG_Y + y}, device_id_type=MESH)
    got_z.wait_recv()
    for i in range(1, ALONG_Y):
        pltpu.make_async_remote_copy(
            src_ref=refs.at[:, pl.ds(y, 1)], dst_ref=refs.at[:, pl.ds(y, 1)], send_sem=day_sems.at[0, 4], recv_sem=day_sems.at[1, 4],
            device_id={"day": z * ALONG_Y + (y + i) % ALONG_Y}, device_id_type=MESH).start()
    got_y = pltpu.make_async_remote_copy(
        src_ref=refs.at[:, 0:ALONG_Y - 1], dst_ref=refs.at[:, 0:ALONG_Y - 1], send_sem=day_sems.at[0, 4], recv_sem=day_sems.at[1, 4],
        device_id={"day": z * ALONG_Y + (y + 1) % ALONG_Y}, device_id_type=MESH)
    got_y.wait_recv()
    for copy in sent:
        copy.wait_send()
    turn_zero.wait_send()
    turn_one.wait_send()
    got_z.wait_send()
    got_y.wait_send()
    home.wait_recv()
    home.wait_send()


def lay_out(back, refs, stacks_hbm, reference_hbm, spread, held, stacks, reference, sems):
    groups = held.shape[0] // 8
    held[...] = refs[...].astype(F32).reshape(groups * 8, 128)
    for tile in range(TILES):
        wide = min(128, LAGS - 128 * tile)
        reference[:, 128 * tile:128 * tile + wide] = held[pl.ds(tile, groups, stride=8), :][:, :wide]
    copies = [pltpu.make_async_copy(reference, reference_hbm, sems.at[2])]
    copies[0].start()
    spread[...] = back[...].astype(F32)
    for day in range(2):
        for tile in range(TILES):
            wide = min(128, LAGS - 128 * tile)
            part = spread[pl.ds(8 * day + tile, groups, stride=BLOCK), :].astype(BF16)
            stacks[day, :, 128 * tile:128 * tile + wide] = part[:, :wide]
        copies.append(pltpu.make_async_copy(stacks.at[day], stacks_hbm.at[day], sems.at[day]))
        copies[-1].start()
    for copy in copies:
        copy.wait()


def per_device(spectra, pair_stations, availability):
    groups = lax.axis_size("day")
    days_here, shard, bins2 = spectra.shape
    stations = shard * lax.axis_size("pair")
    pairs = pair_stations.shape[0]
    table = jnp.asarray(lag_table(bins2 // 2))
    vmem = pl.BlockSpec(memory_space=pltpu.VMEM)
    anywhere = pl.BlockSpec(memory_space=pl.ANY)
    padded = pltpu.VMEM((PAD + groups, 8, 128), F32)
    by_day = pltpu.VMEM((days_here, groups, 8, 128), BF16)
    dma = pltpu.SemaphoreType.DMA
    back, refs = pl.pallas_call(
        functools.partial(kernel, groups, groups * days_here),
        out_shape=(pltpu.VMEM((groups * BLOCK, 128), BF16),
                   pltpu.VMEM((groups // ALONG_Y, ALONG_Y, 8, 128), BF16)),
        in_specs=[anywhere] * 4,
        out_specs=(vmem, vmem),
        scratch_shapes=[
            pltpu.VMEM((days_here, stations, bins2 // 2), BF16),
            pltpu.VMEM((bins2, WIDE), BF16),
            pltpu.VMEM((days_here, pairs, bins2), BF16),
            pltpu.VMEM((days_here, pairs, bins2 // 2), BF16),
            pltpu.VMEM((groups * 8, 128), F32),
            by_day, by_day,
            pltpu.VMEM((groups * BLOCK, 128), BF16),
            pltpu.VMEM((2, 2, pairs), jnp.int32),
            pltpu.VMEM((days_here, stations), jnp.int32),
            padded, padded, padded, padded, padded,
            dma((9,)), dma((18, 2)), dma((18, 2)), dma((2, 5)),
        ],
        compiler_params=pltpu.CompilerParams(
            collective_id=0, has_side_effects=True, vmem_limit_bytes=VMEM_LIMIT),
    )(spectra, pair_stations.T, availability, table)
    return pl.pallas_call(
        lay_out,
        out_shape=(jax.ShapeDtypeStruct((days_here, pairs, LAGS), BF16), jax.ShapeDtypeStruct((pairs, LAGS), F32)),
        in_specs=[vmem, vmem],
        out_specs=(anywhere, anywhere),
        scratch_shapes=[
            pltpu.VMEM((groups * BLOCK, 128), F32),
            pltpu.VMEM((groups * 8, 128), F32),
            pltpu.VMEM((days_here, pairs, LAGS), BF16),
            pltpu.VMEM((pairs, LAGS), F32),
            dma((3,)),
        ],
        compiler_params=pltpu.CompilerParams(vmem_limit_bytes=8 * 2**20),
    )(back, refs)


def solution(mesh):
    return jax.shard_map(
        per_device,
        mesh=mesh,
        in_specs=(P("day", "pair", None), P("pair", None), P("day", None)),
        out_specs=(P("day", "pair", None), P("pair", None)),
        check_vma=False,
    )
```

```python
import functools

import jax
import jax.numpy as jnp
import numpy as np
from jax import lax
from jax.experimental import pallas as pl
from jax.experimental.pallas import tpu as pltpu
from jax.sharding import PartitionSpec as P

LAGS = 1001
WIDE = 1024
TILES = WIDE // 128
WINDOW = 30
ALONG_X = 4
ALONG_Y = 4
BLOCK = 16
PAD = 16
F32 = jnp.float32
BF16 = jnp.bfloat16
MESH = pl.DeviceIdType.MESH
SPOT = LAGS - 128 * (TILES - 1)
VMEM_LIMIT = 58 * 2**20


def lag_table(bin_count):
    bin_ids = np.arange(bin_count)[:, None]
    lag_ids = np.arange(LAGS)[None, :] - (LAGS - 1) // 2
    angle = np.mod(bin_ids * lag_ids, 2 * bin_count) * (np.pi / bin_count)
    factor = 1.0 / np.sqrt(2.0 * bin_count)
    table = np.concatenate([np.cos(angle) * factor, -np.sin(angle) * factor], 0)
    return np.pad(table, ((0, 0), (0, WIDE - LAGS))).astype(np.float32).astype(jnp.bfloat16)


def rows(index, count=BLOCK):
    return pl.ds(pl.multiple_of(index * count, count), count)


def kernel(groups, days, spectra, ends_hbm, availability_hbm, table_hbm, back, refs,
           gathered, table, cross, handed, received, so_far, spread, daily, turned, ready, ends, availability,
           odd_pad, sum_pad, two_pad, four_pad, eight_pad,
           local_sems, give, take, day_sems):
    me = lax.axis_index("day")
    mine = lax.axis_index("pair")
    x, core = mine // 2, mine % 2
    z, y = me // ALONG_Y, me % ALONG_Y
    planes = groups // ALONG_Y
    sibling = x * 2 + 1 - core
    half = spectra.shape[2] // 2
    part = half // 2
    pairs = ends.shape[2]
    far = groups // 2

    barrier = pltpu.get_barrier_semaphore()

    def greet(i, carry):
        for away in (far + i, far - i):
            pl.semaphore_signal(barrier, inc=1, device_id={"day": (me + away) % groups}, device_id_type=MESH)
        return carry

    pl.semaphore_signal(barrier, inc=1, device_id={"day": (me + far) % groups}, device_id_type=MESH)
    lax.fori_loop(1, far // 2, greet, 0)

    def at_offset(step, flip):
        return ((x + step) % ALONG_X) * 2 + (1 - core if flip else core)

    offsets = [(step, flip) for step in (1, 3, 2, 0) for flip in (False, True) if step or flip]
    for step, flip in offsets:
        pl.semaphore_signal(barrier, inc=1, device_id={"pair": at_offset(step, flip)}, device_id_type=MESH)
    lax.fori_loop(far // 2, far, greet, 0)

    def bins(which, kind):
        return pl.ds(pl.multiple_of(which * part + kind * half, 128), part)

    own_copies = []
    for kind in range(2):
        for day in range(2):
            own_copies.append(pltpu.make_async_copy(
                spectra.at[day, :, bins(core, kind)], gathered.at[day, rows(mine), kind * part:(kind + 1) * part],
                local_sems.at[4 + 2 * kind + day]))
            own_copies[-1].start()
    ends_copy = pltpu.make_async_copy(ends_hbm, ends.at[0], local_sems.at[1])
    ends_copy.start()
    availability_copy = pltpu.make_async_copy(availability_hbm, availability, local_sems.at[2])
    availability_copy.start()
    table_copies = []
    for number in range(4):
        from_row = (core if number < 2 else 1 - core) * part + (number % 2) * half
        table_copies.append(pltpu.make_async_copy(
            table_hbm.at[pl.ds(pl.multiple_of(from_row, 128), part)], table.at[number * part:(number + 1) * part],
            local_sems.at[9 + number]))
        table_copies[-1].start()
    for pad in (odd_pad, sum_pad, two_pad, four_pad, eight_pad):
        pad[0:PAD] = jnp.zeros((PAD, 8, 128), F32)
    pl.semaphore_wait(barrier, groups - 1 + len(offsets))

    sent = []

    def to(src, dst, send_sem, recv_sem, other):
        copy = pltpu.make_async_remote_copy(
            src_ref=src, dst_ref=dst, send_sem=send_sem, recv_sem=recv_sem,
            device_id={"pair": other}, device_id_type=MESH)
        copy.start()
        sent.append(copy)
        return copy

    def send_own(day):
        copies = []
        for number, (step, flip) in enumerate(offsets):
            for kind in range(2):
                copies.append(to(
                    spectra.at[day, :, bins(1 - core if flip else core, kind)],
                    gathered.at[day, rows(mine), kind * part:(kind + 1) * part],
                    give.at[2 * number + kind, day], take.at[2 * number + kind, day], at_offset(step, flip)))
        return copies

    def cross_of(day):
        copies = []
        width = min(512, part)
        for number, at in enumerate(range(0, part, width)):
            real = jnp.dot(pick, gathered[day, :, at:at + width], preferred_element_type=F32)
            imag = jnp.dot(pick, gathered[day, :, part + at:part + at + width], preferred_element_type=F32)
            ar, br, ai, bi = real[:2 * pairs], real[2 * pairs:], imag[:2 * pairs], imag[2 * pairs:]
            for kind, made in enumerate(((ar * br + ai * bi).astype(BF16), (ar * bi - ai * br).astype(BF16))):
                place = slice(kind * part + at, kind * part + at + width)
                handed[day, :, place] = made[pairs:]
                cross[day, :, place] = made[:pairs]
                copies.append(to(
                    handed.at[day, :, place], received.at[day, :, place],
                    give.at[14 + 2 * number + kind, day], take.at[14 + 2 * number + kind, day], sibling))
        return copies

    def daily_of(day, copies):
        shown = present[day]
        spare = lax.broadcasted_iota(jnp.int32, (pairs, 128), 1) == SPOT
        for at in range(0, WIDE, 256):
            so_far[:, at:at + 256] = jnp.dot(cross[day], table[0:half, at:at + 256], preferred_element_type=F32)
        for copy in copies:
            copy.wait_recv()
        for at in range(0, WIDE, 256):
            corr = so_far[:, at:at + 256] + jnp.dot(
                received[day], table[half:2 * half, at:at + 256], preferred_element_type=F32)
            for j in range(2):
                tile = at // 128 + j
                piece = corr[:, 128 * j:128 * (j + 1)] * shown
                if tile == TILES - 1:
                    piece = jnp.where(spare, shown, piece)
                spread[pl.ds(tile, pairs, stride=8), :] = piece
        daily[day] = spread[...].reshape(groups, 8, 128).astype(BF16)

    def turn(here, there, send_sem, recv_sem):
        def copy(to_group):
            return pltpu.make_async_remote_copy(
                src_ref=here(to_group, 1), dst_ref=there(me, 1), send_sem=send_sem, recv_sem=recv_sem,
                device_id={"day": to_group}, device_id_type=MESH)

        copy((me + far) % groups).start()

        def step(i, carry):
            copy((me + far + i) % groups).start()
            copy((me + far - i) % groups).start()
            return carry

        lax.fori_loop(1, far, step, 0)
        return pltpu.make_async_remote_copy(
            src_ref=here(0, groups - 1), dst_ref=there(0, groups - 1), send_sem=send_sem, recv_sem=recv_sem,
            device_id={"day": (me + 1) % groups}, device_id_type=MESH)

    def turn_day(day):
        copies = turn(lambda i, n: daily.at[day, pl.ds(i, n)], lambda i, n: turned.at[day, pl.ds(i, n)],
                      day_sems.at[0, day], day_sems.at[1, day])
        turned[day, pl.ds(me, 1)] = daily[day, pl.ds(me, 1)]
        return copies

    own_zero = send_own(0)
    ends_copy.wait()
    met = to(ends.at[0], ends.at[1], local_sems.at[0], local_sems.at[8], sibling)
    availability_copy.wait()
    met.wait_recv()
    station = lax.broadcasted_iota(jnp.int32, (128, pairs), 0)

    def picks(end):
        return [jnp.where(station == ends[who, end:end + 1, :], 1.0, 0.0).astype(F32).T for who in range(2)]

    pick_one, pick_two = picks(0), picks(1)
    pick = jnp.concatenate(pick_one + pick_two, 0).astype(BF16)
    present = []
    for day in range(2):
        up = availability[day:day + 1, :].astype(F32)
        present.append(jnp.sum(pick_one[0] * up, axis=1, keepdims=True) * jnp.sum(pick_two[0] * up, axis=1, keepdims=True))
    for copy in own_zero:
        copy.wait_send()
    sent.clear()
    sent.append(met)
    own_one = send_own(1)
    for copy in own_copies:
        copy.wait()
    for copy in own_zero:
        copy.wait_recv()
    halves_zero = cross_of(0)
    for copy in table_copies:
        copy.wait()
    daily_of(0, halves_zero)
    turn_zero = turn_day(0)
    for copy in own_one:
        copy.wait_recv()
    daily_of(1, cross_of(1))
    turn_one = turn_day(1)
    turn_zero.wait_recv()
    turn_one.wait_recv()

    even, odd = turned[0].astype(F32), turned[1].astype(F32)
    both = even + odd
    ref_row = jnp.sum(both, axis=0) / days
    refs[pl.ds(z, 1), pl.ds(y, 1)] = ref_row.astype(BF16)[None, None]

    def along_z(plane):
        return pltpu.make_async_remote_copy(
            src_ref=refs.at[pl.ds(z, 1), pl.ds(y, 1)], dst_ref=refs.at[pl.ds(z, 1), pl.ds(y, 1)], send_sem=day_sems.at[0, 2], recv_sem=day_sems.at[1, 2],
            device_id={"day": plane * ALONG_Y + y}, device_id_type=MESH)

    def step_z(i, carry):
        along_z((z + i) % planes).start()
        return carry

    lax.fori_loop(1, planes, step_z, 0)
    own = slice(PAD, PAD + groups)

    def past(ref, by):
        return ref[PAD - by:PAD - by + groups]

    odd_pad[own] = odd
    sum_pad[own] = both
    two = both + past(sum_pad, 1)
    two_pad[own] = two
    four = two + past(two_pad, 2)
    four_pad[own] = four
    eight_pad[own] = four + past(four_pad, 4)
    full = past(eight_pad, 1) + past(four_pad, 9) + past(two_pad, 13)
    lag = 128 * lax.broadcasted_iota(jnp.int32, (8, 128), 0) + lax.broadcasted_iota(jnp.int32, (8, 128), 1)
    power = jnp.sum(jnp.where(lag < LAGS, ref_row * ref_row, 0.0), axis=(0, 1), keepdims=True) / LAGS
    scale = jnp.sqrt(power + 1e-06)[None]

    def normalised(moving):
        counts = moving[:, 7:8, SPOT:SPOT + 1]
        return moving * (1.0 / (jnp.maximum(counts, 1.0) * scale))

    ready[...] = jnp.concatenate(
        [normalised(full + past(odd_pad, 15) + even), normalised(full + both)], 1).reshape(groups * BLOCK, 128).astype(BF16)
    home = turn(lambda i, n: ready.at[pl.ds(pl.multiple_of(i * BLOCK, BLOCK), n * BLOCK)],
                lambda i, n: back.at[pl.ds(pl.multiple_of(i * BLOCK, BLOCK), n * BLOCK)],
                day_sems.at[0, 3], day_sems.at[1, 3])
    back[rows(me), :] = ready[rows(me), :]

    got_z = pltpu.make_async_remote_copy(
        src_ref=refs.at[0:planes - 1, 0:1], dst_ref=refs.at[0:planes - 1, 0:1], send_sem=day_sems.at[0, 2], recv_sem=day_sems.at[1, 2],
        device_id={"day": ((z + 1) % planes) * ALONG_Y + y}, device_id_type=MESH)
    got_z.wait_recv()
    for i in range(1, ALONG_Y):
        pltpu.make_async_remote_copy(
            src_ref=refs.at[:, pl.ds(y, 1)], dst_ref=refs.at[:, pl.ds(y, 1)], send_sem=day_sems.at[0, 4], recv_sem=day_sems.at[1, 4],
            device_id={"day": z * ALONG_Y + (y + i) % ALONG_Y}, device_id_type=MESH).start()
    got_y = pltpu.make_async_remote_copy(
        src_ref=refs.at[:, 0:ALONG_Y - 1], dst_ref=refs.at[:, 0:ALONG_Y - 1], send_sem=day_sems.at[0, 4], recv_sem=day_sems.at[1, 4],
        device_id={"day": z * ALONG_Y + (y + 1) % ALONG_Y}, device_id_type=MESH)
    got_y.wait_recv()
    for copy in sent:
        copy.wait_send()
    turn_zero.wait_send()
    turn_one.wait_send()
    got_z.wait_send()
    got_y.wait_send()
    home.wait_recv()
    home.wait_send()


def lay_out(back, refs, stacks_hbm, reference_hbm, spread, held, stacks, reference, sems):
    groups = held.shape[0] // 8
    held[...] = refs[...].astype(F32).reshape(groups * 8, 128)
    for tile in range(TILES):
        wide = min(128, LAGS - 128 * tile)
        reference[:, 128 * tile:128 * tile + wide] = held[pl.ds(tile, groups, stride=8), :][:, :wide]
    copies = [pltpu.make_async_copy(reference, reference_hbm, sems.at[2])]
    copies[0].start()
    spread[...] = back[...].astype(F32)
    for day in range(2):
        for tile in range(TILES):
            wide = min(128, LAGS - 128 * tile)
            part = spread[pl.ds(8 * day + tile, groups, stride=BLOCK), :].astype(BF16)
            stacks[day, :, 128 * tile:128 * tile + wide] = part[:, :wide]
        copies.append(pltpu.make_async_copy(stacks.at[day], stacks_hbm.at[day], sems.at[day]))
        copies[-1].start()
    for copy in copies:
        copy.wait()


def per_device(spectra, pair_stations, availability):
    groups = lax.axis_size("day")
    days_here, shard, bins2 = spectra.shape
    stations = shard * lax.axis_size("pair")
    pairs = pair_stations.shape[0]
    table = jnp.asarray(lag_table(bins2 // 2))
    vmem = pl.BlockSpec(memory_space=pltpu.VMEM)
    anywhere = pl.BlockSpec(memory_space=pl.ANY)
    padded = pltpu.VMEM((PAD + groups, 8, 128), F32)
    by_day = pltpu.VMEM((days_here, groups, 8, 128), BF16)
    dma = pltpu.SemaphoreType.DMA
    back, refs = pl.pallas_call(
        functools.partial(kernel, groups, groups * days_here),
        out_shape=(pltpu.VMEM((groups * BLOCK, 128), BF16),
                   pltpu.VMEM((groups // ALONG_Y, ALONG_Y, 8, 128), BF16)),
        in_specs=[anywhere] * 4,
        out_specs=(vmem, vmem),
        scratch_shapes=[
            pltpu.VMEM((days_here, stations, bins2 // 2), BF16),
            pltpu.VMEM((bins2, WIDE), BF16),
            pltpu.VMEM((days_here, pairs, bins2 // 2), BF16),
            pltpu.VMEM((days_here, pairs, bins2 // 2), BF16),
            pltpu.VMEM((days_here, pairs, bins2 // 2), BF16),
            pltpu.VMEM((pairs, WIDE), F32),
            pltpu.VMEM((groups * 8, 128), F32),
            by_day, by_day,
            pltpu.VMEM((groups * BLOCK, 128), BF16),
            pltpu.VMEM((2, 2, pairs), jnp.int32),
            pltpu.VMEM((days_here, stations), jnp.int32),
            padded, padded, padded, padded, padded,
            dma((13,)), dma((18, 2)), dma((18, 2)), dma((2, 5)),
        ],
        compiler_params=pltpu.CompilerParams(
            collective_id=0, has_side_effects=True, vmem_limit_bytes=VMEM_LIMIT),
    )(spectra, pair_stations.T, availability, table)
    return pl.pallas_call(
        lay_out,
        out_shape=(jax.ShapeDtypeStruct((days_here, pairs, LAGS), BF16), jax.ShapeDtypeStruct((pairs, LAGS), F32)),
        in_specs=[vmem, vmem],
        out_specs=(anywhere, anywhere),
        scratch_shapes=[
            pltpu.VMEM((groups * BLOCK, 128), F32),
            pltpu.VMEM((groups * 8, 128), F32),
            pltpu.VMEM((days_here, pairs, LAGS), BF16),
            pltpu.VMEM((pairs, LAGS), F32),
            dma((3,)),
        ],
        compiler_params=pltpu.CompilerParams(vmem_limit_bytes=8 * 2**20),
    )(back, refs)


def solution(mesh):
    return jax.shard_map(
        per_device,
        mesh=mesh,
        in_specs=(P("day", "pair", None), P("pair", None), P("day", None)),
        out_specs=(P("day", "pair", None), P("pair", None)),
        check_vma=False,
    )
```

```python
import functools

import jax
import jax.numpy as jnp
import numpy as np
from jax import lax
from jax.experimental import pallas as pl
from jax.experimental.pallas import tpu as pltpu
from jax.sharding import PartitionSpec as P

LAGS = 1001
WIDE = 1024
TILES = WIDE // 128
WINDOW = 30
ALONG_X = 4
ALONG_Y = 4
BLOCK = 16
PAD = 16
F32 = jnp.float32
BF16 = jnp.bfloat16
MESH = pl.DeviceIdType.MESH
SPOT = LAGS - 128 * (TILES - 1)
VMEM_LIMIT = 58 * 2**20


def lag_table(bin_count):
    bin_ids = np.arange(bin_count)[:, None]
    lag_ids = np.arange(LAGS)[None, :] - (LAGS - 1) // 2
    angle = np.mod(bin_ids * lag_ids, 2 * bin_count) * (np.pi / bin_count)
    factor = 1.0 / np.sqrt(2.0 * bin_count)
    table = np.concatenate([np.cos(angle) * factor, -np.sin(angle) * factor], 0)
    return np.pad(table, ((0, 0), (0, WIDE - LAGS))).astype(np.float32).astype(jnp.bfloat16)


def rows(index, count=BLOCK):
    return pl.ds(pl.multiple_of(index * count, count), count)


def kernel(groups, days, spectra, ends_hbm, availability_hbm, table_hbm, back, refs,
           gathered, table, cross, handed, received, so_far, spread, daily, turned, ready, ends, availability,
           odd_pad, sum_pad, two_pad, four_pad, eight_pad,
           local_sems, give, take, day_sems):
    me = lax.axis_index("day")
    mine = lax.axis_index("pair")
    x, core = mine // 2, mine % 2
    z, y = me // ALONG_Y, me % ALONG_Y
    planes = groups // ALONG_Y
    sibling = x * 2 + 1 - core
    half = spectra.shape[2] // 2
    part = half // 2
    pairs = ends.shape[2]
    far = groups // 2

    barrier = pltpu.get_barrier_semaphore()

    def greet(i, carry):
        for away in (far + i, far - i):
            pl.semaphore_signal(barrier, inc=1, device_id={"day": (me + away) % groups}, device_id_type=MESH)
        return carry

    pl.semaphore_signal(barrier, inc=1, device_id={"day": (me + far) % groups}, device_id_type=MESH)
    lax.fori_loop(1, far // 2, greet, 0)

    def at_offset(step, flip):
        return ((x + step) % ALONG_X) * 2 + (1 - core if flip else core)

    offsets = [(step, flip) for step in (1, 3, 2, 0) for flip in (False, True) if step or flip]
    for step, flip in offsets:
        pl.semaphore_signal(barrier, inc=1, device_id={"pair": at_offset(step, flip)}, device_id_type=MESH)
    lax.fori_loop(far // 2, far, greet, 0)

    def bins(which, kind):
        return pl.ds(pl.multiple_of(which * part + kind * half, 128), part)

    own_copies = []
    for kind in range(2):
        for day in range(2):
            own_copies.append(pltpu.make_async_copy(
                spectra.at[day, :, bins(core, kind)], gathered.at[day, rows(mine), kind * part:(kind + 1) * part],
                local_sems.at[4 + 2 * kind + day]))
            own_copies[-1].start()
    ends_copy = pltpu.make_async_copy(ends_hbm, ends.at[0], local_sems.at[1])
    ends_copy.start()
    availability_copy = pltpu.make_async_copy(availability_hbm, availability, local_sems.at[2])
    availability_copy.start()
    table_copies = []
    for number in range(4):
        from_row = (core if number < 2 else 1 - core) * part + (number % 2) * half
        table_copies.append(pltpu.make_async_copy(
            table_hbm.at[pl.ds(pl.multiple_of(from_row, 128), part)], table.at[number * part:(number + 1) * part],
            local_sems.at[9 + number]))
        table_copies[-1].start()
    for pad in (odd_pad, sum_pad, two_pad, four_pad, eight_pad):
        pad[0:PAD] = jnp.zeros((PAD, 8, 128), F32)
    pl.semaphore_wait(barrier, groups - 1 + len(offsets))

    sent = []

    def to(src, dst, send_sem, recv_sem, other):
        copy = pltpu.make_async_remote_copy(
            src_ref=src, dst_ref=dst, send_sem=send_sem, recv_sem=recv_sem,
            device_id={"pair": other}, device_id_type=MESH)
        copy.start()
        sent.append(copy)
        return copy

    def send_own(day):
        copies = []
        for number, (step, flip) in enumerate(offsets):
            for kind in range(2):
                copies.append(to(
                    spectra.at[day, :, bins(1 - core if flip else core, kind)],
                    gathered.at[day, rows(mine), kind * part:(kind + 1) * part],
                    give.at[2 * number + kind, day], take.at[2 * number + kind, day], at_offset(step, flip)))
        return copies

    def cross_of(day):
        copies = []
        width = min(1024, part)
        for number, at in enumerate(range(0, part, width)):
            real = jnp.dot(pick, gathered[day, :, at:at + width], preferred_element_type=F32)
            imag = jnp.dot(pick, gathered[day, :, part + at:part + at + width], preferred_element_type=F32)
            ar, br, ai, bi = real[:2 * pairs], real[2 * pairs:], imag[:2 * pairs], imag[2 * pairs:]
            for kind, made in enumerate(((ar * br + ai * bi).astype(BF16), (ar * bi - ai * br).astype(BF16))):
                place = slice(kind * part + at, kind * part + at + width)
                handed[day, :, place] = made[pairs:]
                cross[day, :, place] = made[:pairs]
                copies.append(to(
                    handed.at[day, :, place], received.at[day, :, place],
                    give.at[14 + 2 * number + kind, day], take.at[14 + 2 * number + kind, day], sibling))
        return copies

    def daily_of(day, copies):
        shown = present[day]
        spare = lax.broadcasted_iota(jnp.int32, (pairs, 128), 1) == SPOT
        for at in range(0, WIDE, 256):
            so_far[:, at:at + 256] = jnp.dot(cross[day], table[0:half, at:at + 256], preferred_element_type=F32)
        for copy in copies:
            copy.wait_recv()
        for at in range(0, WIDE, 256):
            corr = so_far[:, at:at + 256] + jnp.dot(
                received[day], table[half:2 * half, at:at + 256], preferred_element_type=F32)
            for j in range(2):
                tile = at // 128 + j
                piece = corr[:, 128 * j:128 * (j + 1)] * shown
                if tile == TILES - 1:
                    piece = jnp.where(spare, shown, piece)
                spread[pl.ds(tile, pairs, stride=8), :] = piece
        daily[day] = spread[...].reshape(groups, 8, 128).astype(BF16)

    def turn(here, there, send_sem, recv_sem):
        def copy(to_group):
            return pltpu.make_async_remote_copy(
                src_ref=here(to_group, 1), dst_ref=there(me, 1), send_sem=send_sem, recv_sem=recv_sem,
                device_id={"day": to_group}, device_id_type=MESH)

        copy((me + far) % groups).start()

        def step(i, carry):
            copy((me + far + i) % groups).start()
            copy((me + far - i) % groups).start()
            return carry

        lax.fori_loop(1, far, step, 0)
        return pltpu.make_async_remote_copy(
            src_ref=here(0, groups - 1), dst_ref=there(0, groups - 1), send_sem=send_sem, recv_sem=recv_sem,
            device_id={"day": (me + 1) % groups}, device_id_type=MESH)

    def turn_day(day):
        copies = turn(lambda i, n: daily.at[day, pl.ds(i, n)], lambda i, n: turned.at[day, pl.ds(i, n)],
                      day_sems.at[0, day], day_sems.at[1, day])
        turned[day, pl.ds(me, 1)] = daily[day, pl.ds(me, 1)]
        return copies

    own_zero = send_own(0)
    ends_copy.wait()
    met = to(ends.at[0], ends.at[1], local_sems.at[0], local_sems.at[8], sibling)
    availability_copy.wait()
    met.wait_recv()
    station = lax.broadcasted_iota(jnp.int32, (128, pairs), 0)

    def picks(end):
        return [jnp.where(station == ends[who, end:end + 1, :], 1.0, 0.0).astype(F32).T for who in range(2)]

    pick_one, pick_two = picks(0), picks(1)
    pick = jnp.concatenate(pick_one + pick_two, 0).astype(BF16)
    present = []
    for day in range(2):
        up = availability[day:day + 1, :].astype(F32)
        present.append(jnp.sum(pick_one[0] * up, axis=1, keepdims=True) * jnp.sum(pick_two[0] * up, axis=1, keepdims=True))
    for copy in own_zero:
        copy.wait_send()
    sent.clear()
    sent.append(met)
    own_one = send_own(1)
    for copy in own_copies:
        copy.wait()
    for copy in own_zero:
        copy.wait_recv()
    halves_zero = cross_of(0)
    for copy in table_copies:
        copy.wait()
    daily_of(0, halves_zero)
    turn_zero = turn_day(0)
    for copy in own_one:
        copy.wait_recv()
    daily_of(1, cross_of(1))
    turn_one = turn_day(1)
    turn_zero.wait_recv()
    turn_one.wait_recv()

    even, odd = turned[0].astype(F32), turned[1].astype(F32)
    both = even + odd
    ref_row = jnp.sum(both, axis=0) / days
    refs[pl.ds(z, 1), pl.ds(y, 1)] = ref_row.astype(BF16)[None, None]

    def along_z(plane):
        return pltpu.make_async_remote_copy(
            src_ref=refs.at[pl.ds(z, 1), pl.ds(y, 1)], dst_ref=refs.at[pl.ds(z, 1), pl.ds(y, 1)], send_sem=day_sems.at[0, 2], recv_sem=day_sems.at[1, 2],
            device_id={"day": plane * ALONG_Y + y}, device_id_type=MESH)

    def step_z(i, carry):
        along_z((z + i) % planes).start()
        return carry

    lax.fori_loop(1, planes, step_z, 0)
    own = slice(PAD, PAD + groups)

    def past(ref, by):
        return ref[PAD - by:PAD - by + groups]

    odd_pad[own] = odd
    sum_pad[own] = both
    two = both + past(sum_pad, 1)
    two_pad[own] = two
    four = two + past(two_pad, 2)
    four_pad[own] = four
    eight_pad[own] = four + past(four_pad, 4)
    full = past(eight_pad, 1) + past(four_pad, 9) + past(two_pad, 13)
    lag = 128 * lax.broadcasted_iota(jnp.int32, (8, 128), 0) + lax.broadcasted_iota(jnp.int32, (8, 128), 1)
    power = jnp.sum(jnp.where(lag < LAGS, ref_row * ref_row, 0.0), axis=(0, 1), keepdims=True) / LAGS
    scale = jnp.sqrt(power + 1e-06)[None]

    def normalised(moving):
        counts = moving[:, 7:8, SPOT:SPOT + 1]
        return moving * (1.0 / (jnp.maximum(counts, 1.0) * scale))

    ready[...] = jnp.concatenate(
        [normalised(full + past(odd_pad, 15) + even), normalised(full + both)], 1).reshape(groups * BLOCK, 128).astype(BF16)
    home = turn(lambda i, n: ready.at[pl.ds(pl.multiple_of(i * BLOCK, BLOCK), n * BLOCK)],
                lambda i, n: back.at[pl.ds(pl.multiple_of(i * BLOCK, BLOCK), n * BLOCK)],
                day_sems.at[0, 3], day_sems.at[1, 3])
    back[rows(me), :] = ready[rows(me), :]

    got_z = pltpu.make_async_remote_copy(
        src_ref=refs.at[0:planes - 1, 0:1], dst_ref=refs.at[0:planes - 1, 0:1], send_sem=day_sems.at[0, 2], recv_sem=day_sems.at[1, 2],
        device_id={"day": ((z + 1) % planes) * ALONG_Y + y}, device_id_type=MESH)
    got_z.wait_recv()
    for i in range(1, ALONG_Y):
        pltpu.make_async_remote_copy(
            src_ref=refs.at[:, pl.ds(y, 1)], dst_ref=refs.at[:, pl.ds(y, 1)], send_sem=day_sems.at[0, 4], recv_sem=day_sems.at[1, 4],
            device_id={"day": z * ALONG_Y + (y + i) % ALONG_Y}, device_id_type=MESH).start()
    got_y = pltpu.make_async_remote_copy(
        src_ref=refs.at[:, 0:ALONG_Y - 1], dst_ref=refs.at[:, 0:ALONG_Y - 1], send_sem=day_sems.at[0, 4], recv_sem=day_sems.at[1, 4],
        device_id={"day": z * ALONG_Y + (y + 1) % ALONG_Y}, device_id_type=MESH)
    got_y.wait_recv()
    for copy in sent:
        copy.wait_send()
    turn_zero.wait_send()
    turn_one.wait_send()
    got_z.wait_send()
    got_y.wait_send()
    home.wait_recv()
    home.wait_send()


def lay_out(back, refs, stacks_hbm, reference_hbm, spread, held, stacks, reference, sems):
    groups = held.shape[0] // 8
    held[...] = refs[...].astype(F32).reshape(groups * 8, 128)
    for tile in range(TILES):
        wide = min(128, LAGS - 128 * tile)
        reference[:, 128 * tile:128 * tile + wide] = held[pl.ds(tile, groups, stride=8), :][:, :wide]
    copies = [pltpu.make_async_copy(reference, reference_hbm, sems.at[2])]
    copies[0].start()
    spread[...] = back[...].astype(F32)
    for day in range(2):
        for tile in range(TILES):
            wide = min(128, LAGS - 128 * tile)
            part = spread[pl.ds(8 * day + tile, groups, stride=BLOCK), :].astype(BF16)
            stacks[day, :, 128 * tile:128 * tile + wide] = part[:, :wide]
        copies.append(pltpu.make_async_copy(stacks.at[day], stacks_hbm.at[day], sems.at[day]))
        copies[-1].start()
    for copy in copies:
        copy.wait()


def per_device(spectra, pair_stations, availability):
    groups = lax.axis_size("day")
    days_here, shard, bins2 = spectra.shape
    stations = shard * lax.axis_size("pair")
    pairs = pair_stations.shape[0]
    table = jnp.asarray(lag_table(bins2 // 2))
    vmem = pl.BlockSpec(memory_space=pltpu.VMEM)
    anywhere = pl.BlockSpec(memory_space=pl.ANY)
    padded = pltpu.VMEM((PAD + groups, 8, 128), F32)
    by_day = pltpu.VMEM((days_here, groups, 8, 128), BF16)
    dma = pltpu.SemaphoreType.DMA
    back, refs = pl.pallas_call(
        functools.partial(kernel, groups, groups * days_here),
        out_shape=(pltpu.VMEM((groups * BLOCK, 128), BF16),
                   pltpu.VMEM((groups // ALONG_Y, ALONG_Y, 8, 128), BF16)),
        in_specs=[anywhere] * 4,
        out_specs=(vmem, vmem),
        scratch_shapes=[
            pltpu.VMEM((days_here, stations, bins2 // 2), BF16),
            pltpu.VMEM((bins2, WIDE), BF16),
            pltpu.VMEM((days_here, pairs, bins2 // 2), BF16),
            pltpu.VMEM((days_here, pairs, bins2 // 2), BF16),
            pltpu.VMEM((days_here, pairs, bins2 // 2), BF16),
            pltpu.VMEM((pairs, WIDE), F32),
            pltpu.VMEM((groups * 8, 128), F32),
            by_day, by_day,
            pltpu.VMEM((groups * BLOCK, 128), BF16),
            pltpu.VMEM((2, 2, pairs), jnp.int32),
            pltpu.VMEM((days_here, stations), jnp.int32),
            padded, padded, padded, padded, padded,
            dma((13,)), dma((18, 2)), dma((18, 2)), dma((2, 5)),
        ],
        compiler_params=pltpu.CompilerParams(
            collective_id=0, has_side_effects=True, vmem_limit_bytes=VMEM_LIMIT),
    )(spectra, pair_stations.T, availability, table)
    return pl.pallas_call(
        lay_out,
        out_shape=(jax.ShapeDtypeStruct((days_here, pairs, LAGS), BF16), jax.ShapeDtypeStruct((pairs, LAGS), F32)),
        in_specs=[vmem, vmem],
        out_specs=(anywhere, anywhere),
        scratch_shapes=[
            pltpu.VMEM((groups * BLOCK, 128), F32),
            pltpu.VMEM((groups * 8, 128), F32),
            pltpu.VMEM((days_here, pairs, LAGS), BF16),
            pltpu.VMEM((pairs, LAGS), F32),
            dma((3,)),
        ],
        compiler_params=pltpu.CompilerParams(vmem_limit_bytes=8 * 2**20),
    )(back, refs)


def solution(mesh):
    return jax.shard_map(
        per_device,
        mesh=mesh,
        in_specs=(P("day", "pair", None), P("pair", None), P("day", None)),
        out_specs=(P("day", "pair", None), P("pair", None)),
        check_vma=False,
    )
```

```python
import functools

import jax
import jax.numpy as jnp
import numpy as np
from jax import lax
from jax.experimental import pallas as pl
from jax.experimental.pallas import tpu as pltpu
from jax.sharding import PartitionSpec as P

LAGS = 1001
WIDE = 1024
TILES = WIDE // 128
WINDOW = 30
ALONG_X = 4
ALONG_Y = 4
BLOCK = 16
PAD = 16
F32 = jnp.float32
BF16 = jnp.bfloat16
MESH = pl.DeviceIdType.MESH
SPOT = LAGS - 128 * (TILES - 1)
VMEM_LIMIT = 58 * 2**20


def lag_table(bin_count):
    bin_ids = np.arange(bin_count)[:, None]
    lag_ids = np.arange(LAGS)[None, :] - (LAGS - 1) // 2
    angle = np.mod(bin_ids * lag_ids, 2 * bin_count) * (np.pi / bin_count)
    factor = 1.0 / np.sqrt(2.0 * bin_count)
    table = np.concatenate([np.cos(angle) * factor, -np.sin(angle) * factor], 0)
    return np.pad(table, ((0, 0), (0, WIDE - LAGS))).astype(np.float32).astype(jnp.bfloat16)


def rows(index, count=BLOCK):
    return pl.ds(pl.multiple_of(index * count, count), count)


def kernel(groups, days, spectra, ends_hbm, availability_hbm, table_hbm, back, reference,
           gathered, table, cross, handed, received, so_far, spread, daily, turned, ready, ends, availability,
           odd_pad, sum_pad, two_pad, four_pad, eight_pad, refs,
           local_sems, give, take, day_sems):
    me = lax.axis_index("day")
    mine = lax.axis_index("pair")
    x, core = mine // 2, mine % 2
    z, y = me // ALONG_Y, me % ALONG_Y
    planes = groups // ALONG_Y
    sibling = x * 2 + 1 - core
    half = spectra.shape[2] // 2
    part = half // 2
    pairs = ends.shape[2]
    far = groups // 2

    barrier = pltpu.get_barrier_semaphore()

    def greet(i, carry):
        for away in (far + i, far - i):
            pl.semaphore_signal(barrier, inc=1, device_id={"day": (me + away) % groups}, device_id_type=MESH)
        return carry

    pl.semaphore_signal(barrier, inc=1, device_id={"day": (me + far) % groups}, device_id_type=MESH)
    lax.fori_loop(1, far // 2, greet, 0)

    def at_offset(step, flip):
        return ((x + step) % ALONG_X) * 2 + (1 - core if flip else core)

    offsets = [(step, flip) for step in (1, 3, 2, 0) for flip in (False, True) if step or flip]
    for step, flip in offsets:
        pl.semaphore_signal(barrier, inc=1, device_id={"pair": at_offset(step, flip)}, device_id_type=MESH)
    lax.fori_loop(far // 2, far, greet, 0)

    def bins(which, kind):
        return pl.ds(pl.multiple_of(which * part + kind * half, 128), part)

    own_copies = []
    for kind in range(2):
        for day in range(2):
            own_copies.append(pltpu.make_async_copy(
                spectra.at[day, :, bins(core, kind)], gathered.at[day, rows(mine), kind * part:(kind + 1) * part],
                local_sems.at[4 + 2 * kind + day]))
            own_copies[-1].start()
    ends_copy = pltpu.make_async_copy(ends_hbm, ends.at[0], local_sems.at[1])
    ends_copy.start()
    availability_copy = pltpu.make_async_copy(availability_hbm, availability, local_sems.at[2])
    availability_copy.start()
    table_copies = []
    for number in range(4):
        from_row = (core if number < 2 else 1 - core) * part + (number % 2) * half
        table_copies.append(pltpu.make_async_copy(
            table_hbm.at[pl.ds(pl.multiple_of(from_row, 128), part)], table.at[number * part:(number + 1) * part],
            local_sems.at[9 + number]))
        table_copies[-1].start()
    for pad in (odd_pad, sum_pad, two_pad, four_pad, eight_pad):
        pad[0:PAD] = jnp.zeros((PAD, 8, 128), F32)
    pl.semaphore_wait(barrier, groups - 1 + len(offsets))

    sent = []

    def to(src, dst, send_sem, recv_sem, other):
        copy = pltpu.make_async_remote_copy(
            src_ref=src, dst_ref=dst, send_sem=send_sem, recv_sem=recv_sem,
            device_id={"pair": other}, device_id_type=MESH)
        copy.start()
        sent.append(copy)
        return copy

    def send_own(day):
        copies = []
        for number, (step, flip) in enumerate(offsets):
            for kind in range(2):
                copies.append(to(
                    spectra.at[day, :, bins(1 - core if flip else core, kind)],
                    gathered.at[day, rows(mine), kind * part:(kind + 1) * part],
                    give.at[2 * number + kind, day], take.at[2 * number + kind, day], at_offset(step, flip)))
        return copies

    def cross_of(day):
        copies = []
        width = min(1024, part)
        for number, at in enumerate(range(0, part, width)):
            real = jnp.dot(pick, gathered[day, :, at:at + width], preferred_element_type=F32)
            imag = jnp.dot(pick, gathered[day, :, part + at:part + at + width], preferred_element_type=F32)
            ar, br, ai, bi = real[:2 * pairs], real[2 * pairs:], imag[:2 * pairs], imag[2 * pairs:]
            for kind, made in enumerate(((ar * br + ai * bi).astype(BF16), (ar * bi - ai * br).astype(BF16))):
                place = slice(kind * part + at, kind * part + at + width)
                handed[day, :, place] = made[pairs:]
                cross[day, :, place] = made[:pairs]
                copies.append(to(
                    handed.at[day, :, place], received.at[day, :, place],
                    give.at[14 + 2 * number + kind, day], take.at[14 + 2 * number + kind, day], sibling))
        return copies

    def daily_of(day, copies):
        shown = present[day]
        spare = lax.broadcasted_iota(jnp.int32, (pairs, 128), 1) == SPOT
        for at in range(0, WIDE, 256):
            so_far[:, at:at + 256] = jnp.dot(cross[day], table[0:half, at:at + 256], preferred_element_type=F32)
        for copy in copies:
            copy.wait_recv()
        for at in range(0, WIDE, 256):
            corr = so_far[:, at:at + 256] + jnp.dot(
                received[day], table[half:2 * half, at:at + 256], preferred_element_type=F32)
            for j in range(2):
                tile = at // 128 + j
                piece = corr[:, 128 * j:128 * (j + 1)] * shown
                if tile == TILES - 1:
                    piece = jnp.where(spare, shown, piece)
                spread[pl.ds(tile, pairs, stride=8), :] = piece
        daily[day] = spread[...].reshape(groups, 8, 128).astype(BF16)

    def turn(here, there, send_sem, recv_sem):
        def copy(to_group):
            return pltpu.make_async_remote_copy(
                src_ref=here(to_group, 1), dst_ref=there(me, 1), send_sem=send_sem, recv_sem=recv_sem,
                device_id={"day": to_group}, device_id_type=MESH)

        copy((me + far) % groups).start()

        def step(i, carry):
            copy((me + far + i) % groups).start()
            copy((me + far - i) % groups).start()
            return carry

        lax.fori_loop(1, far, step, 0)
        return pltpu.make_async_remote_copy(
            src_ref=here(0, groups - 1), dst_ref=there(0, groups - 1), send_sem=send_sem, recv_sem=recv_sem,
            device_id={"day": (me + 1) % groups}, device_id_type=MESH)

    def turn_day(day):
        copies = turn(lambda i, n: daily.at[day, pl.ds(i, n)], lambda i, n: turned.at[day, pl.ds(i, n)],
                      day_sems.at[0, day], day_sems.at[1, day])
        turned[day, pl.ds(me, 1)] = daily[day, pl.ds(me, 1)]
        return copies

    own_zero = send_own(0)
    ends_copy.wait()
    met = to(ends.at[0], ends.at[1], local_sems.at[0], local_sems.at[8], sibling)
    availability_copy.wait()
    met.wait_recv()
    station = lax.broadcasted_iota(jnp.int32, (128, pairs), 0)

    def picks(end):
        return [jnp.where(station == ends[who, end:end + 1, :], 1.0, 0.0).astype(F32).T for who in range(2)]

    pick_one, pick_two = picks(0), picks(1)
    pick = jnp.concatenate(pick_one + pick_two, 0).astype(BF16)
    present = []
    for day in range(2):
        up = availability[day:day + 1, :].astype(F32)
        present.append(jnp.sum(pick_one[0] * up, axis=1, keepdims=True) * jnp.sum(pick_two[0] * up, axis=1, keepdims=True))
    for copy in own_zero:
        copy.wait_send()
    sent.clear()
    sent.append(met)
    own_one = send_own(1)
    for copy in own_copies:
        copy.wait()
    for copy in own_zero:
        copy.wait_recv()
    halves_zero = cross_of(0)
    for copy in table_copies:
        copy.wait()
    daily_of(0, halves_zero)
    turn_zero = turn_day(0)
    for copy in own_one:
        copy.wait_recv()
    daily_of(1, cross_of(1))
    turn_one = turn_day(1)
    turn_zero.wait_recv()
    turn_one.wait_recv()

    even, odd = turned[0].astype(F32), turned[1].astype(F32)
    both = even + odd
    ref_row = jnp.sum(both, axis=0) / days
    refs[pl.ds(z, 1), pl.ds(y, 1)] = ref_row.astype(BF16)[None, None]

    def along_z(plane):
        return pltpu.make_async_remote_copy(
            src_ref=refs.at[pl.ds(z, 1), pl.ds(y, 1)], dst_ref=refs.at[pl.ds(z, 1), pl.ds(y, 1)], send_sem=day_sems.at[0, 2], recv_sem=day_sems.at[1, 2],
            device_id={"day": plane * ALONG_Y + y}, device_id_type=MESH)

    def step_z(i, carry):
        along_z((z + i) % planes).start()
        return carry

    lax.fori_loop(1, planes, step_z, 0)
    own = slice(PAD, PAD + groups)

    def past(ref, by):
        return ref[PAD - by:PAD - by + groups]

    odd_pad[own] = odd
    sum_pad[own] = both
    two = both + past(sum_pad, 1)
    two_pad[own] = two
    four = two + past(two_pad, 2)
    four_pad[own] = four
    eight_pad[own] = four + past(four_pad, 4)
    full = past(eight_pad, 1) + past(four_pad, 9) + past(two_pad, 13)
    lag = 128 * lax.broadcasted_iota(jnp.int32, (8, 128), 0) + lax.broadcasted_iota(jnp.int32, (8, 128), 1)
    power = jnp.sum(jnp.where(lag < LAGS, ref_row * ref_row, 0.0), axis=(0, 1), keepdims=True) / LAGS
    scale = jnp.sqrt(power + 1e-06)[None]

    def normalised(moving):
        counts = moving[:, 7:8, SPOT:SPOT + 1]
        return moving * (1.0 / (jnp.maximum(counts, 1.0) * scale))

    ready[...] = jnp.concatenate(
        [normalised(full + past(odd_pad, 15) + even), normalised(full + both)], 1).reshape(groups * BLOCK, 128).astype(BF16)
    home = turn(lambda i, n: ready.at[pl.ds(pl.multiple_of(i * BLOCK, BLOCK), n * BLOCK)],
                lambda i, n: back.at[pl.ds(pl.multiple_of(i * BLOCK, BLOCK), n * BLOCK)],
                day_sems.at[0, 3], day_sems.at[1, 3])
    back[rows(me), :] = ready[rows(me), :]

    got_z = pltpu.make_async_remote_copy(
        src_ref=refs.at[0:planes - 1, 0:1], dst_ref=refs.at[0:planes - 1, 0:1], send_sem=day_sems.at[0, 2], recv_sem=day_sems.at[1, 2],
        device_id={"day": ((z + 1) % planes) * ALONG_Y + y}, device_id_type=MESH)
    got_z.wait_recv()
    for i in range(1, ALONG_Y):
        pltpu.make_async_remote_copy(
            src_ref=refs.at[:, pl.ds(y, 1)], dst_ref=refs.at[:, pl.ds(y, 1)], send_sem=day_sems.at[0, 4], recv_sem=day_sems.at[1, 4],
            device_id={"day": z * ALONG_Y + (y + i) % ALONG_Y}, device_id_type=MESH).start()
    got_y = pltpu.make_async_remote_copy(
        src_ref=refs.at[:, 0:ALONG_Y - 1], dst_ref=refs.at[:, 0:ALONG_Y - 1], send_sem=day_sems.at[0, 4], recv_sem=day_sems.at[1, 4],
        device_id={"day": z * ALONG_Y + (y + 1) % ALONG_Y}, device_id_type=MESH)
    got_y.wait_recv()
    spread[...] = refs[...].astype(F32).reshape(groups * 8, 128)
    for tile in range(TILES):
        wide = min(128, LAGS - 128 * tile)
        reference[:, 128 * tile:128 * tile + wide] = spread[pl.ds(tile, groups, stride=8), :][:, :wide]
    for copy in sent:
        copy.wait_send()
    turn_zero.wait_send()
    turn_one.wait_send()
    got_z.wait_send()
    got_y.wait_send()
    home.wait_recv()
    home.wait_send()


def lay_out(back, reference, stacks_hbm, reference_hbm, spread, stacks, sems):
    groups = back.shape[0] // BLOCK
    copies = [pltpu.make_async_copy(reference, reference_hbm, sems.at[2])]
    copies[0].start()
    spread[...] = back[...].astype(F32)
    for day in range(2):
        for tile in range(TILES):
            wide = min(128, LAGS - 128 * tile)
            part = spread[pl.ds(8 * day + tile, groups, stride=BLOCK), :].astype(BF16)
            stacks[day, :, 128 * tile:128 * tile + wide] = part[:, :wide]
        copies.append(pltpu.make_async_copy(stacks.at[day], stacks_hbm.at[day], sems.at[day]))
        copies[-1].start()
    for copy in copies:
        copy.wait()


def per_device(spectra, pair_stations, availability):
    groups = lax.axis_size("day")
    days_here, shard, bins2 = spectra.shape
    stations = shard * lax.axis_size("pair")
    pairs = pair_stations.shape[0]
    table = jnp.asarray(lag_table(bins2 // 2))
    vmem = pl.BlockSpec(memory_space=pltpu.VMEM)
    anywhere = pl.BlockSpec(memory_space=pl.ANY)
    padded = pltpu.VMEM((PAD + groups, 8, 128), F32)
    by_day = pltpu.VMEM((days_here, groups, 8, 128), BF16)
    dma = pltpu.SemaphoreType.DMA
    back, reference = pl.pallas_call(
        functools.partial(kernel, groups, groups * days_here),
        out_shape=(pltpu.VMEM((groups * BLOCK, 128), BF16),
                   pltpu.VMEM((pairs, LAGS), F32)),
        in_specs=[anywhere] * 4,
        out_specs=(vmem, vmem),
        scratch_shapes=[
            pltpu.VMEM((days_here, stations, bins2 // 2), BF16),
            pltpu.VMEM((bins2, WIDE), BF16),
            pltpu.VMEM((days_here, pairs, bins2 // 2), BF16),
            pltpu.VMEM((days_here, pairs, bins2 // 2), BF16),
            pltpu.VMEM((days_here, pairs, bins2 // 2), BF16),
            pltpu.VMEM((pairs, WIDE), F32),
            pltpu.VMEM((groups * 8, 128), F32),
            by_day, by_day,
            pltpu.VMEM((groups * BLOCK, 128), BF16),
            pltpu.VMEM((2, 2, pairs), jnp.int32),
            pltpu.VMEM((days_here, stations), jnp.int32),
            padded, padded, padded, padded, padded,
            pltpu.VMEM((groups // ALONG_Y, ALONG_Y, 8, 128), BF16),
            dma((13,)), dma((18, 2)), dma((18, 2)), dma((2, 5)),
        ],
        compiler_params=pltpu.CompilerParams(
            collective_id=0, has_side_effects=True, vmem_limit_bytes=VMEM_LIMIT),
    )(spectra, pair_stations.T, availability, table)
    return pl.pallas_call(
        lay_out,
        out_shape=(jax.ShapeDtypeStruct((days_here, pairs, LAGS), BF16), jax.ShapeDtypeStruct((pairs, LAGS), F32)),
        in_specs=[vmem, vmem],
        out_specs=(anywhere, anywhere),
        scratch_shapes=[
            pltpu.VMEM((groups * BLOCK, 128), F32),
            pltpu.VMEM((days_here, pairs, LAGS), BF16),
            dma((3,)),
        ],
        compiler_params=pltpu.CompilerParams(vmem_limit_bytes=8 * 2**20),
    )(back, reference)


def solution(mesh):
    return jax.shard_map(
        per_device,
        mesh=mesh,
        in_specs=(P("day", "pair", None), P("pair", None), P("day", None)),
        out_specs=(P("day", "pair", None), P("pair", None)),
        check_vma=False,
    )
```

```python
import functools

import jax
import jax.numpy as jnp
import numpy as np
from jax import lax
from jax.experimental import pallas as pl
from jax.experimental.pallas import tpu as pltpu
from jax.sharding import PartitionSpec as P

LAGS = 1001
WIDE = 1024
TILES = WIDE // 128
WINDOW = 30
ALONG_X = 4
ALONG_Y = 4
BLOCK = 16
PAD = 16
F32 = jnp.float32
BF16 = jnp.bfloat16
MESH = pl.DeviceIdType.MESH
SPOT = LAGS - 128 * (TILES - 1)
VMEM_LIMIT = 58 * 2**20


def lag_table(bin_count):
    bin_ids = np.arange(bin_count)[:, None]
    lag_ids = np.arange(LAGS)[None, :] - (LAGS - 1) // 2
    angle = np.mod(bin_ids * lag_ids, 2 * bin_count) * (np.pi / bin_count)
    factor = 1.0 / np.sqrt(2.0 * bin_count)
    table = np.concatenate([np.cos(angle) * factor, -np.sin(angle) * factor], 0)
    return np.pad(table, ((0, 0), (0, WIDE - LAGS))).astype(np.float32).astype(jnp.bfloat16)


def rows(index, count=BLOCK):
    return pl.ds(pl.multiple_of(index * count, count), count)


def kernel(groups, days, spectra, ends_hbm, availability_hbm, table_hbm, back, reference,
           gathered, table, cross, handed, received, so_far, spread, daily, turned, ready, ends, availability,
           odd_pad, sum_pad, two_pad, four_pad, eight_pad, refs,
           local_sems, give, take, day_sems):
    me = lax.axis_index("day")
    mine = lax.axis_index("pair")
    x, core = mine // 2, mine % 2
    z, y = me // ALONG_Y, me % ALONG_Y
    planes = groups // ALONG_Y
    sibling = x * 2 + 1 - core
    half = spectra.shape[2] // 2
    part = half // 2
    pairs = ends.shape[2]
    far = groups // 2

    barrier = pltpu.get_barrier_semaphore()

    def greet(i, carry):
        for away in (far + i, far - i):
            pl.semaphore_signal(barrier, inc=1, device_id={"day": (me + away) % groups}, device_id_type=MESH)
        return carry

    pl.semaphore_signal(barrier, inc=1, device_id={"day": (me + far) % groups}, device_id_type=MESH)
    lax.fori_loop(1, far // 2, greet, 0)

    def at_offset(step, flip):
        return ((x + step) % ALONG_X) * 2 + (1 - core if flip else core)

    offsets = [(step, flip) for step in (1, 3, 2, 0) for flip in (False, True) if step or flip]
    for step, flip in offsets:
        pl.semaphore_signal(barrier, inc=1, device_id={"pair": at_offset(step, flip)}, device_id_type=MESH)
    lax.fori_loop(far // 2, far, greet, 0)

    def bins(which, kind):
        return pl.ds(pl.multiple_of(which * part + kind * half, 128), part)

    own_copies = []
    for kind in range(2):
        for day in range(2):
            own_copies.append(pltpu.make_async_copy(
                spectra.at[day, :, bins(core, kind)], gathered.at[day, rows(mine), kind * part:(kind + 1) * part],
                local_sems.at[4 + 2 * kind + day]))
            own_copies[-1].start()
    ends_copy = pltpu.make_async_copy(ends_hbm, ends.at[0], local_sems.at[1])
    ends_copy.start()
    availability_copy = pltpu.make_async_copy(availability_hbm, availability, local_sems.at[2])
    availability_copy.start()
    table_copies = []
    for number in range(4):
        from_row = (core if number < 2 else 1 - core) * part + (number % 2) * half
        table_copies.append(pltpu.make_async_copy(
            table_hbm.at[pl.ds(pl.multiple_of(from_row, 128), part)], table.at[number * part:(number + 1) * part],
            local_sems.at[9 + number]))
        table_copies[-1].start()
    for pad in (odd_pad, sum_pad, two_pad, four_pad, eight_pad):
        pad[0:PAD] = jnp.zeros((PAD, 8, 128), F32)
    pl.semaphore_wait(barrier, groups - 1 + len(offsets))

    sent = []

    def to(src, dst, send_sem, recv_sem, other):
        copy = pltpu.make_async_remote_copy(
            src_ref=src, dst_ref=dst, send_sem=send_sem, recv_sem=recv_sem,
            device_id={"pair": other}, device_id_type=MESH)
        copy.start()
        sent.append(copy)
        return copy

    def send_own(day):
        copies = []
        for number, (step, flip) in enumerate(offsets):
            for kind in range(2):
                copies.append(to(
                    spectra.at[day, :, bins(1 - core if flip else core, kind)],
                    gathered.at[day, rows(mine), kind * part:(kind + 1) * part],
                    give.at[2 * number + kind, day], take.at[2 * number + kind, day], at_offset(step, flip)))
        return copies

    def cross_of(day):
        copies = []
        width = min(1024, part)
        for number, at in enumerate(range(0, part, width)):
            real = jnp.dot(pick, gathered[day, :, at:at + width], preferred_element_type=F32)
            imag = jnp.dot(pick, gathered[day, :, part + at:part + at + width], preferred_element_type=F32)
            ar, br, ai, bi = real[:2 * pairs], real[2 * pairs:], imag[:2 * pairs], imag[2 * pairs:]
            for kind, made in enumerate(((ar * br + ai * bi).astype(BF16), (ar * bi - ai * br).astype(BF16))):
                place = slice(kind * part + at, kind * part + at + width)
                handed[day, :, place] = made[pairs:]
                cross[day, :, place] = made[:pairs]
                copies.append(to(
                    handed.at[day, :, place], received.at[day, :, place],
                    give.at[14 + 2 * number + kind, day], take.at[14 + 2 * number + kind, day], sibling))
        return copies

    def daily_of(day, copies):
        shown = present[day]
        spare = lax.broadcasted_iota(jnp.int32, (pairs, 128), 1) == SPOT
        for at in range(0, WIDE, 256):
            so_far[:, at:at + 256] = jnp.dot(cross[day], table[0:half, at:at + 256], preferred_element_type=F32)
        for copy in copies:
            copy.wait_recv()
        for at in range(0, WIDE, 256):
            corr = so_far[:, at:at + 256] + jnp.dot(
                received[day], table[half:2 * half, at:at + 256], preferred_element_type=F32)
            for j in range(2):
                tile = at // 128 + j
                piece = corr[:, 128 * j:128 * (j + 1)] * shown
                if tile == TILES - 1:
                    piece = jnp.where(spare, shown, piece)
                spread[pl.ds(tile, pairs, stride=8), :] = piece
        daily[day] = spread[...].reshape(groups, 8, 128).astype(BF16)

    def turn(here, there, send_sem, recv_sem):
        def copy(to_group):
            return pltpu.make_async_remote_copy(
                src_ref=here(to_group, 1), dst_ref=there(me, 1), send_sem=send_sem, recv_sem=recv_sem,
                device_id={"day": to_group}, device_id_type=MESH)

        copy((me + far) % groups).start()

        def step(i, carry):
            copy((me + far + i) % groups).start()
            copy((me + far - i) % groups).start()
            return carry

        lax.fori_loop(1, far, step, 0)
        return pltpu.make_async_remote_copy(
            src_ref=here(0, groups - 1), dst_ref=there(0, groups - 1), send_sem=send_sem, recv_sem=recv_sem,
            device_id={"day": (me + 1) % groups}, device_id_type=MESH)

    def turn_day(day):
        copies = turn(lambda i, n: daily.at[day, pl.ds(i, n)], lambda i, n: turned.at[day, pl.ds(i, n)],
                      day_sems.at[0, day], day_sems.at[1, day])
        turned[day, pl.ds(me, 1)] = daily[day, pl.ds(me, 1)]
        return copies

    own_zero = send_own(0)
    ends_copy.wait()
    met = to(ends.at[0], ends.at[1], local_sems.at[0], local_sems.at[8], sibling)
    availability_copy.wait()
    met.wait_recv()
    station = lax.broadcasted_iota(jnp.int32, (128, pairs), 0)

    def picks(end):
        return [jnp.where(station == ends[who, end:end + 1, :], 1.0, 0.0).astype(F32).T for who in range(2)]

    pick_one, pick_two = picks(0), picks(1)
    pick = jnp.concatenate(pick_one + pick_two, 0).astype(BF16)
    present = []
    for day in range(2):
        up = availability[day:day + 1, :].astype(F32)
        present.append(jnp.sum(pick_one[0] * up, axis=1, keepdims=True) * jnp.sum(pick_two[0] * up, axis=1, keepdims=True))
    for copy in own_zero:
        copy.wait_send()
    sent.clear()
    sent.append(met)
    own_one = send_own(1)
    for copy in own_copies:
        copy.wait()
    for copy in own_zero:
        copy.wait_recv()
    halves_zero = cross_of(0)
    for copy in table_copies:
        copy.wait()
    daily_of(0, halves_zero)
    turn_zero = turn_day(0)
    for copy in own_one:
        copy.wait_recv()
    daily_of(1, cross_of(1))
    turn_one = turn_day(1)
    turn_zero.wait_recv()
    turn_one.wait_recv()

    even, odd = turned[0].astype(F32), turned[1].astype(F32)
    both = even + odd
    ref_row = jnp.sum(both, axis=0) / days
    refs[pl.ds(z, 1), pl.ds(y, 1)] = ref_row.astype(BF16)[None, None]

    def along_z(plane):
        return pltpu.make_async_remote_copy(
            src_ref=refs.at[pl.ds(z, 1), pl.ds(y, 1)], dst_ref=refs.at[pl.ds(z, 1), pl.ds(y, 1)], send_sem=day_sems.at[0, 2], recv_sem=day_sems.at[1, 2],
            device_id={"day": plane * ALONG_Y + y}, device_id_type=MESH)

    def step_z(i, carry):
        along_z((z + i) % planes).start()
        return carry

    lax.fori_loop(1, planes, step_z, 0)
    own = slice(PAD, PAD + groups)

    def past(ref, by):
        return ref[PAD - by:PAD - by + groups]

    odd_pad[own] = odd
    sum_pad[own] = both
    two = both + past(sum_pad, 1)
    two_pad[own] = two
    four = two + past(two_pad, 2)
    four_pad[own] = four
    eight_pad[own] = four + past(four_pad, 4)
    full = past(eight_pad, 1) + past(four_pad, 9) + past(two_pad, 13)
    lag = 128 * lax.broadcasted_iota(jnp.int32, (8, 128), 0) + lax.broadcasted_iota(jnp.int32, (8, 128), 1)
    power = jnp.sum(jnp.where(lag < LAGS, ref_row * ref_row, 0.0), axis=(0, 1), keepdims=True) / LAGS
    scale = jnp.sqrt(power + 1e-06)[None]

    def normalised(moving):
        counts = moving[:, 7:8, SPOT:SPOT + 1]
        return moving * (1.0 / (jnp.maximum(counts, 1.0) * scale))

    ready[...] = jnp.concatenate(
        [normalised(full + past(odd_pad, 15) + even), normalised(full + both)], 1).reshape(groups * BLOCK, 128).astype(BF16)
    home = turn(lambda i, n: ready.at[pl.ds(pl.multiple_of(i * BLOCK, BLOCK), n * BLOCK)],
                lambda i, n: back.at[pl.ds(pl.multiple_of(i * BLOCK, BLOCK), n * BLOCK)],
                day_sems.at[0, 3], day_sems.at[1, 3])
    back[rows(me), :] = ready[rows(me), :]

    got_z = pltpu.make_async_remote_copy(
        src_ref=refs.at[0:planes - 1, 0:1], dst_ref=refs.at[0:planes - 1, 0:1], send_sem=day_sems.at[0, 2], recv_sem=day_sems.at[1, 2],
        device_id={"day": ((z + 1) % planes) * ALONG_Y + y}, device_id_type=MESH)
    got_z.wait_recv()
    for i in range(1, ALONG_Y):
        pltpu.make_async_remote_copy(
            src_ref=refs.at[:, pl.ds(y, 1)], dst_ref=refs.at[:, pl.ds(y, 1)], send_sem=day_sems.at[0, 4], recv_sem=day_sems.at[1, 4],
            device_id={"day": z * ALONG_Y + (y + i) % ALONG_Y}, device_id_type=MESH).start()
    got_y = pltpu.make_async_remote_copy(
        src_ref=refs.at[:, 0:ALONG_Y - 1], dst_ref=refs.at[:, 0:ALONG_Y - 1], send_sem=day_sems.at[0, 4], recv_sem=day_sems.at[1, 4],
        device_id={"day": z * ALONG_Y + (y + 1) % ALONG_Y}, device_id_type=MESH)
    got_y.wait_recv()
    spread[...] = refs[...].astype(F32).reshape(groups * 8, 128)
    for tile in range(TILES):
        wide = min(128, LAGS - 128 * tile)
        reference[:, 128 * tile:128 * tile + wide] = spread[pl.ds(tile, groups, stride=8), :][:, :wide]
    for copy in sent:
        copy.wait_send()
    turn_zero.wait_send()
    turn_one.wait_send()
    got_z.wait_send()
    got_y.wait_send()
    home.wait_recv()
    home.wait_send()


def lay_out(back, reference, stacks_hbm, reference_hbm, spread, stacks, sems):
    groups = back.shape[0] // BLOCK
    copies = [pltpu.make_async_copy(reference, reference_hbm, sems.at[2])]
    copies[0].start()
    share = groups // 2
    for number in range(2):
        own = slice(number * share, (number + 1) * share)
        base = number * share * BLOCK
        spread[base:base + share * BLOCK] = back[base:base + share * BLOCK].astype(F32)
        for day in range(2):
            for tile in range(TILES):
                wide = min(128, LAGS - 128 * tile)
                part = spread[pl.ds(base + 8 * day + tile, share, stride=BLOCK), :].astype(BF16)
                stacks[day, own, 128 * tile:128 * tile + wide] = part[:, :wide]
        copies.append(pltpu.make_async_copy(stacks.at[:, own], stacks_hbm.at[:, own], sems.at[number]))
        copies[-1].start()
    for copy in copies:
        copy.wait()


def per_device(spectra, pair_stations, availability):
    groups = lax.axis_size("day")
    days_here, shard, bins2 = spectra.shape
    stations = shard * lax.axis_size("pair")
    pairs = pair_stations.shape[0]
    table = jnp.asarray(lag_table(bins2 // 2))
    vmem = pl.BlockSpec(memory_space=pltpu.VMEM)
    anywhere = pl.BlockSpec(memory_space=pl.ANY)
    padded = pltpu.VMEM((PAD + groups, 8, 128), F32)
    by_day = pltpu.VMEM((days_here, groups, 8, 128), BF16)
    dma = pltpu.SemaphoreType.DMA
    back, reference = pl.pallas_call(
        functools.partial(kernel, groups, groups * days_here),
        out_shape=(pltpu.VMEM((groups * BLOCK, 128), BF16),
                   pltpu.VMEM((pairs, LAGS), F32)),
        in_specs=[anywhere] * 4,
        out_specs=(vmem, vmem),
        scratch_shapes=[
            pltpu.VMEM((days_here, stations, bins2 // 2), BF16),
            pltpu.VMEM((bins2, WIDE), BF16),
            pltpu.VMEM((days_here, pairs, bins2 // 2), BF16),
            pltpu.VMEM((days_here, pairs, bins2 // 2), BF16),
            pltpu.VMEM((days_here, pairs, bins2 // 2), BF16),
            pltpu.VMEM((pairs, WIDE), F32),
            pltpu.VMEM((groups * 8, 128), F32),
            by_day, by_day,
            pltpu.VMEM((groups * BLOCK, 128), BF16),
            pltpu.VMEM((2, 2, pairs), jnp.int32),
            pltpu.VMEM((days_here, stations), jnp.int32),
            padded, padded, padded, padded, padded,
            pltpu.VMEM((groups // ALONG_Y, ALONG_Y, 8, 128), BF16),
            dma((13,)), dma((18, 2)), dma((18, 2)), dma((2, 5)),
        ],
        compiler_params=pltpu.CompilerParams(
            collective_id=0, has_side_effects=True, vmem_limit_bytes=VMEM_LIMIT),
    )(spectra, pair_stations.T, availability, table)
    return pl.pallas_call(
        lay_out,
        out_shape=(jax.ShapeDtypeStruct((days_here, pairs, LAGS), BF16), jax.ShapeDtypeStruct((pairs, LAGS), F32)),
        in_specs=[vmem, vmem],
        out_specs=(anywhere, anywhere),
        scratch_shapes=[
            pltpu.VMEM((groups * BLOCK, 128), F32),
            pltpu.VMEM((days_here, pairs, LAGS), BF16),
            dma((3,)),
        ],
        compiler_params=pltpu.CompilerParams(vmem_limit_bytes=8 * 2**20),
    )(back, reference)


def solution(mesh):
    return jax.shard_map(
        per_device,
        mesh=mesh,
        in_specs=(P("day", "pair", None), P("pair", None), P("day", None)),
        out_specs=(P("day", "pair", None), P("pair", None)),
        check_vma=False,
    )
```
